32 devices in a mesh: gx: 8 (over z, y), gy: 4 (over x, core).
Axes of the slice: x: 2, y: 2, z: 4, core: 2. Of those that a mesh axis runs over, the one named last changes fastest.
Arguments:
- flux_perturbation: float32 [2, 4096, 4096], P(None, 'gx', 'gy'), may hold values from -6 to 6
- archived_nominal_heat_levels: float32 [2, 2, 4096, 4096], P(None, None, 'gx', 'gy'), may hold values from -4 to 4
- archived_solidity_labels: int32 [2, 2, 4096, 4096], P(None, None, 'gx', 'gy'), may hold values from 0 to 2
Outputs:
- hess_vec: float32 [2, 4096, 4096], P(None, 'gx', 'gy')
The draws below stay inside these ranges and needn't reach their ends.
Inputs may be any that keep to these rules, and one draw needn't show every extreme that they name: `archived_solidity_labels`: 0 is solid, 1 mushy, 2 liquid.
All inputs are finite; a program needn't handle non-finite values.
Results may differ from the reference program's by a relative error of at most 0.000061.
Values sent between devices are 32-bit elements; how exact they have to be, the bound alone decides.
A program may use at most 192 MiB of HBM per device.

```python
import math
import jax
import jax.numpy as jnp
from jax import lax

NVEC = 2
MESH_LENGTHWISE = 4096
MESH_TRANSVERSE = 4096
SUBSURFACE_TIERS = 2
ARCHIVED_MOMENTS = 2


def draw_flux_perturbation(key, part):
    keys = jax.random.split(key, 4)
    modes = 4
    low_x = MESH_LENGTHWISE // 384 + 1
    high_x = MESH_LENGTHWISE // 64 + 1
    low_y = MESH_TRANSVERSE // 384 + 1
    high_y = MESH_TRANSVERSE // 64 + 1
    freq_x = jax.random.randint(keys[0], (NVEC, 3, modes), low_x, high_x)
    freq_y = jax.random.randint(keys[1], (NVEC, 3, modes), low_y, high_y)
    phase = jax.random.uniform(keys[2], (NVEC, 3, modes), jnp.float32, 0.0, 2.0 * math.pi)
    pos_x = jnp.arange(MESH_LENGTHWISE, dtype=jnp.int32)
    pos_y = jnp.arange(MESH_TRANSVERSE, dtype=jnp.int32)
    angle_x = (freq_x[..., None] * pos_x % MESH_LENGTHWISE).astype(jnp.float32) * (2.0 * math.pi / MESH_LENGTHWISE) + phase[..., None]
    angle_y = (freq_y[..., None] * pos_y % MESH_TRANSVERSE).astype(jnp.float32) * (2.0 * math.pi / MESH_TRANSVERSE)
    cos_x = jnp.cos(angle_x)
    sin_x = jnp.sin(angle_x)
    cos_y = jnp.cos(angle_y)
    sin_y = jnp.sin(angle_y)
    sign_x = (1 - 2 * (pos_x % 2)).astype(jnp.float32)
    sign_y = (1 - 2 * (pos_y % 2)).astype(jnp.float32)
    unit_x = jnp.ones((MESH_LENGTHWISE,), jnp.float32)
    unit_y = jnp.ones((MESH_TRANSVERSE,), jnp.float32)
    base = jax.random.normal(keys[3], (NVEC, MESH_LENGTHWISE, MESH_TRANSVERSE), jnp.float32)
    amplitude = 1.5
    weight = amplitude * math.sqrt(2.0 / modes)
    pattern_x = (sign_x, unit_x, sign_x)
    pattern_y = (unit_y, sign_y, sign_y)
    total = base
    for pattern in range(3):
        envelope = jnp.zeros((NVEC, MESH_LENGTHWISE, MESH_TRANSVERSE), jnp.float32)
        for mode in range(modes):
            envelope = envelope + cos_x[:, pattern, mode][:, :, None] * cos_y[:, pattern, mode][:, None, :]
            envelope = envelope - sin_x[:, pattern, mode][:, :, None] * sin_y[:, pattern, mode][:, None, :]
        total = total + weight * envelope * pattern_x[pattern][None, :, None] * pattern_y[pattern][None, None, :]
    return jnp.clip(total, -6.0, 6.0).astype(jnp.float32)


def place_ends(drawn, stream_key, smallest, largest):
    longest = drawn.shape.index(max(drawn.shape))
    spots = []
    for shift in (0, 1):
        where = [jax.random.randint(jax.random.fold_in(stream_key, axis), (), 0, length) for axis, length in enumerate(drawn.shape)]
        where[longest] = (where[longest] + shift) % drawn.shape[longest]
        spots.append(tuple(where))
    return drawn.at[spots[0]].set(smallest).at[spots[1]].set(largest)


def levels(key, shape, cuts, low, high):
    loudness, own = 1.0, jax.random.fold_in(key, 6)
    for position, blocks in cuts:
        draws = jnp.exp(jax.random.uniform(jax.random.fold_in(own, position), (blocks,), jnp.float32, low / len(cuts), high / len(cuts)))
        loudness = loudness * jnp.repeat(draws, shape[position] // blocks).reshape([-1 if axis == position else 1 for axis in range(len(shape))])
    return loudness


def scatter_about(rng, dims, scale, most, cuts=(), kind=jnp.bfloat16):
    result = scale * jax.random.normal(rng, dims, jnp.float32)
    if cuts:
        result = result * levels(rng, dims, cuts, -0.22, 0.18)
    return jnp.clip(result, -most, most).astype(kind)


def setup_inputs(seed: int = 0) -> dict:
    key_list = jax.random.split(jax.random.key(seed), 4)
    return {
        "flux_perturbation": draw_flux_perturbation(jax.random.fold_in(key_list[3], 71), 0),
        "archived_nominal_heat_levels": scatter_about(key_list[1], (ARCHIVED_MOMENTS, SUBSURFACE_TIERS, MESH_LENGTHWISE, MESH_TRANSVERSE), 1.0, 4.0, ((2, 8), (3, 4)), jnp.float32),
        "archived_solidity_labels": place_ends(jax.random.randint(key_list[2], (ARCHIVED_MOMENTS, SUBSURFACE_TIERS, MESH_LENGTHWISE, MESH_TRANSVERSE), 0, 3), jax.random.fold_in(key_list[2], 1), 0, 2).astype(jnp.int32),
    }


TIME_STEP = 0.1
OBS_WEIGHT = 10.0
PRIOR_GAIN = 0.005


def laplace(field):
    padded = jnp.pad(field, 1)
    total = padded[2:, 1:-1, 1:-1] + padded[:-2, 1:-1, 1:-1]
    total = total + padded[1:-1, 2:, 1:-1] + padded[1:-1, :-2, 1:-1]
    total = total + padded[1:-1, 1:-1, 2:] + padded[1:-1, 1:-1, :-2]
    return total - 6.0 * field


def reference(flux_perturbation, archived_nominal_heat_levels, archived_solidity_labels):
    capacity = jnp.where(archived_solidity_labels == 0, 1.0, jnp.where(archived_solidity_labels == 1, 4.0, 1.25)).astype(jnp.float32)
    diffusion_advance = jnp.where(archived_solidity_labels == 0, 1.0, jnp.where(archived_solidity_labels == 1, 0.6, 0.35)).astype(jnp.float32)
    diffusion_advance = diffusion_advance * (1.0 + 0.5 * jnp.tanh(archived_nominal_heat_levels))
    wave_x = (2.0 * math.pi * jnp.fft.fftfreq(MESH_LENGTHWISE)) ** 2
    wave_y = (2.0 * math.pi * jnp.fft.fftfreq(MESH_TRANSVERSE)) ** 2
    symbol = PRIOR_GAIN * (wave_x[:, None] + wave_y[None, :]) ** 2

    def single(vector):
        zero_layer = jnp.zeros_like(vector)
        source = jnp.stack([vector, zero_layer])
        first_h = TIME_STEP * source
        second_h = first_h + TIME_STEP * (diffusion_advance[0] * laplace(first_h / capacity[0]) + source)
        third_h = second_h + TIME_STEP * (diffusion_advance[1] * laplace(second_h / capacity[1]) + source)
        misfit = OBS_WEIGHT * third_h[0] / capacity[1, 0]
        adj_three = jnp.stack([misfit / capacity[1, 0], zero_layer])
        adj_two = adj_three + laplace(TIME_STEP * diffusion_advance[1] * adj_three) / capacity[1]
        adj_one = adj_two + laplace(TIME_STEP * diffusion_advance[0] * adj_two) / capacity[0]
        data_term = TIME_STEP * (adj_three[0] + adj_two[0] + adj_one[0])
        prior_term = jnp.real(jnp.fft.ifft2(jnp.fft.fft2(vector) * symbol))
        return (data_term + prior_term).astype(jnp.float32)

    return lax.map(single, flux_perturbation)
```

```python
import math

import jax
import jax.numpy as jnp
import numpy as np
from jax import lax
from jax.experimental import pallas as pl
from jax.experimental.pallas import tpu as pltpu
from jax.sharding import PartitionSpec as P

TIME_STEP = 0.1
OBS_WEIGHT = 10.0
PRIOR_GAIN = 0.005
HIGHEST = lax.Precision.HIGHEST


def with_halo(cells, sides, width):
    for axis, dim in sides:
        count = lax.axis_size(axis)
        ends = count - 1
        head = lax.slice_in_dim(cells, 0, width, axis=dim)
        tail = lax.slice_in_dim(cells, cells.shape[dim] - width, cells.shape[dim], axis=dim)
        cells = jnp.concatenate(
            [
                lax.ppermute(tail, axis, [(i, (i + 1) % count) for i in range(ends)]),
                cells,
                lax.ppermute(head, axis, [((i + 1) % count, i) for i in range(ends)]),
            ],
            axis=dim,
        )
    return cells


def surface_rim(field):
    padded = with_halo(field, (("gx", 1), ("gy", 2)), 1)
    return padded[:, 2:, 1:-1] + padded[:, :-2, 1:-1] + padded[:, 1:-1, 2:] + padded[:, 1:-1, :-2]


def cos_sin(horizontal_line_total, col_count, modulus):
    row_ids = jnp.arange(horizontal_line_total, dtype=jnp.int32)[:, None]
    col_ids = jnp.arange(col_count, dtype=jnp.int32)[None, :]
    angles = (row_ids * col_ids % modulus).astype(jnp.float32) * (2.0 * math.pi / modulus)
    return (jnp.cos(angles), jnp.sin(angles))


def tables(length):
    bit_count = length.bit_length() - 1
    outer_len = 2 ** (bit_count // 2)
    inner_len = length // outer_len
    cos_outer, sin_outer = cos_sin(outer_len, outer_len, outer_len)
    cos_inner, sin_inner = cos_sin(inner_len, inner_len, inner_len)
    twist_cos, twist_sin = cos_sin(outer_len, inner_len, length)
    outer_fwd = jnp.stack([cos_outer, -sin_outer])
    inner_fwd = jnp.stack([jnp.stack([cos_inner, -sin_inner]), jnp.stack([sin_inner, cos_inner])])
    inner_inv = jnp.stack([jnp.stack([cos_inner, sin_inner]), jnp.stack([-sin_inner, cos_inner])])
    outer_inv = jnp.stack([cos_outer, -sin_outer])
    freq_index = (
        jnp.arange(outer_len, dtype=jnp.int32)[:, None]
        + outer_len * jnp.arange(inner_len, dtype=jnp.int32)[None, :]
    )
    signed = jnp.where(freq_index < length // 2, freq_index, freq_index - length).astype(
        jnp.float32
    )
    wave_sq = (signed * (2.0 * math.pi / length)) ** 2
    return (
        length,
        outer_len,
        inner_len,
        outer_fwd,
        inner_fwd,
        inner_inv,
        outer_inv,
        twist_cos,
        twist_sin,
        wave_sq,
    )


def forward(field, table):
    (
        length,
        outer_len,
        inner_len,
        outer_fwd,
        inner_fwd,
        inner_inv,
        outer_inv,
        twist_cos,
        twist_sin,
        wave_sq,
    ) = table
    grid = field.reshape(field.shape[:-1] + (outer_len, inner_len))
    stepped = jnp.einsum("...ab,rak->...rkb", grid, outer_fwd, precision=HIGHEST)
    step_re = stepped[..., 0, :, :]
    step_im = stepped[..., 1, :, :]
    twisted = jnp.stack(
        [step_re * twist_cos + step_im * twist_sin, step_im * twist_cos - step_re * twist_sin],
        axis=-3,
    )
    spec = jnp.einsum("...rkb,rsbm->...skm", twisted, inner_fwd, precision=HIGHEST)
    return (spec[..., 0, :, :], spec[..., 1, :, :])


def inverse(spec_re, spec_im, table):
    (
        length,
        outer_len,
        inner_len,
        outer_fwd,
        inner_fwd,
        inner_inv,
        outer_inv,
        twist_cos,
        twist_sin,
        wave_sq,
    ) = table
    stacked = jnp.stack([spec_re, spec_im], axis=-3)
    halved = jnp.einsum("...skm,srbm->...rkb", stacked, inner_inv, precision=HIGHEST)
    half_re = halved[..., 0, :, :]
    half_im = halved[..., 1, :, :]
    turned = jnp.stack(
        [half_re * twist_cos - half_im * twist_sin, half_im * twist_cos + half_re * twist_sin],
        axis=-3,
    )
    grid = jnp.einsum("...rkb,rka->...ab", turned, outer_inv, precision=HIGHEST)
    return grid.reshape(grid.shape[:-2] + (length,)) / length


def shards_general(flux_perturbation, archived_nominal_heat_levels, archived_solidity_labels):
    capacity = jnp.where(
        archived_solidity_labels == 0, 1.0, jnp.where(archived_solidity_labels == 1, 4.0, 1.25)
    ).astype(jnp.float32)
    diffusion_advance = jnp.where(
        archived_solidity_labels == 0, 1.0, jnp.where(archived_solidity_labels == 1, 0.6, 0.35)
    ).astype(jnp.float32)
    diffusion_advance = diffusion_advance * (1.0 + 0.5 * jnp.tanh(archived_nominal_heat_levels))
    rows = lax.all_to_all(flux_perturbation, "gx", split_axis=2, concat_axis=1, tiled=True)
    row_table = tables(rows.shape[1])
    first_u = TIME_STEP * flux_perturbation / capacity[0, 0]
    second_top = TIME_STEP * flux_perturbation + TIME_STEP * (
        diffusion_advance[0, 0] * (surface_rim(first_u) - 6.0 * first_u) + flux_perturbation
    )
    second_low = TIME_STEP * diffusion_advance[0, 1] * first_u
    top_u = second_top / capacity[1, 0]
    low_u = second_low / capacity[1, 1]
    third_top = second_top + TIME_STEP * (
        diffusion_advance[1, 0] * (surface_rim(top_u) - 6.0 * top_u + low_u) + flux_perturbation
    )
    misfit = OBS_WEIGHT * third_top / capacity[1, 0]
    adj_three = misfit / capacity[1, 0]
    push_top = TIME_STEP * diffusion_advance[1, 0] * adj_three
    adj_two_top = adj_three + (surface_rim(push_top) - 6.0 * push_top) / capacity[1, 0]
    adj_two_low = push_top / capacity[1, 1]
    pull_top = TIME_STEP * diffusion_advance[0, 0] * adj_two_top
    pull_low = TIME_STEP * diffusion_advance[0, 1] * adj_two_low
    adj_one_top = adj_two_top + (surface_rim(pull_top) - 6.0 * pull_top + pull_low) / capacity[0, 0]
    data_term = TIME_STEP * (adj_three + adj_two_top + adj_one_top)
    row_re, row_im = forward(jnp.swapaxes(rows, 1, 2), row_table)
    wave_x = row_table[-1]
    second_x = jnp.swapaxes(
        inverse(2.0 * PRIOR_GAIN * wave_x * row_re, 2.0 * PRIOR_GAIN * wave_x * row_im, row_table),
        1,
        2,
    )
    fourth_x = jnp.swapaxes(
        inverse(
            PRIOR_GAIN * wave_x * wave_x * row_re, PRIOR_GAIN * wave_x * wave_x * row_im, row_table
        ),
        1,
        2,
    )
    second_back, fourth_part = (
        lax.all_to_all(second_x, "gx", split_axis=1, concat_axis=2, tiled=True),
        lax.all_to_all(fourth_x, "gx", split_axis=1, concat_axis=2, tiled=True),
    )
    cols_dir, cols_second = (
        lax.all_to_all(flux_perturbation, "gy", split_axis=1, concat_axis=2, tiled=True),
        lax.all_to_all(second_back, "gy", split_axis=1, concat_axis=2, tiled=True),
    )
    col_table = tables(cols_dir.shape[2])
    dir_re, dir_im = forward(cols_dir, col_table)
    sec_re, sec_im = forward(cols_second, col_table)
    wave_y = col_table[-1]
    mixed = inverse(
        PRIOR_GAIN * wave_y * wave_y * dir_re + wave_y * sec_re,
        PRIOR_GAIN * wave_y * wave_y * dir_im + wave_y * sec_im,
        col_table,
    )
    mixed_back = lax.all_to_all(mixed, "gy", split_axis=2, concat_axis=1, tiled=True)
    return data_term + fourth_part + mixed_back


OUTER = 16


def half_spectrum(xs):
    n = len(xs)
    if n == 2:
        return [(xs[0] + xs[1], None), (xs[0] - xs[1], None)]
    even, odd = half_spectrum(xs[0::2]), half_spectrum(xs[1::2])
    out = [None] * (n // 2 + 1)
    for k in range(n // 4 + 1):
        er, ei = even[k]
        orr, oi = odd[k]
        if k == 0:
            out[0] = (er + orr, None)
            out[n // 2] = (er - orr, None)
        elif k == n // 4:
            out[k] = (er, -orr)
        else:
            c, s = math.cos(2 * math.pi * k / n), math.sin(2 * math.pi * k / n)
            if 8 * k == n:
                tr, ti = c * (orr + oi), c * (oi - orr)
            else:
                tr, ti = c * orr + s * oi, c * oi - s * orr
            out[k] = (er + tr, ei + ti)
            out[n // 2 - k] = (er - tr, ti - ei)
    return out


def half_spectrum_t(gs):
    half = len(gs) - 1
    n = 2 * half
    if n == 2:
        return [gs[0][0] + gs[1][0], gs[0][0] - gs[1][0]]
    even, odd = [], []
    for m in range(n // 4 + 1):
        gr, gi = gs[m]
        if m == 0:
            hr = gs[half][0]
            even.append((gr + hr, None))
            odd.append((gr - hr, None))
        elif m == n // 4:
            even.append((gr, None))
            odd.append((-gi, None))
        else:
            hr, hi = gs[half - m]
            even.append((gr + hr, gi - hi))
            dr, di = gr - hr, gi + hi
            c, s = math.cos(2 * math.pi * m / n), math.sin(2 * math.pi * m / n)
            if 8 * m == n:
                odd.append((c * (dr - di), c * (dr + di)))
            else:
                odd.append((c * dr - s * di, c * di + s * dr))
    out = [None] * n
    out[0::2] = half_spectrum_t(even)
    out[1::2] = half_spectrum_t(odd)
    return out


def line_tables(length):
    inner = length // OUTER
    groups = OUTER // 2
    b = np.arange(inner)[:, None]
    mats = np.zeros((groups, 2 * inner, 2 * inner))
    freq = np.zeros((groups, 2 * inner), np.int64)
    scale = math.sqrt(2.0 / length)
    for k1 in range(1, groups):
        k = k1 + OUTER * np.arange(inner)
        angle = 2.0 * math.pi * ((b * k[None, :]) % length) / length
        c, s = np.cos(angle) * scale, np.sin(angle) * scale
        mats[k1 - 1] = np.block([[c, -s], [s, c]])
        freq[k1 - 1] = np.concatenate([k, k])
    last = groups - 1
    for part, first in ((0, 0), (1, groups)):
        k = first + OUTER * np.arange(inner // 2)
        angle = 2.0 * math.pi * ((b * k[None, :]) % length) / length
        c, s = np.cos(angle) * scale, np.sin(angle) * scale
        k_sin = k.copy()
        if first == 0:
            c[:, 0] = math.sqrt(1.0 / length)
            k_sin[0] = length // 2
            s[:, 0] = -math.sqrt(1.0 / length) * (1 - 2 * (np.arange(inner) % 2))
        span = slice(part * inner, (part + 1) * inner)
        mats[last][span, span] = np.concatenate([c, -s], axis=1)
        freq[last][span] = np.concatenate([k, k_sin])
    signed = np.where(freq < length // 2, freq, freq - length)
    wave = (signed * (2.0 * math.pi / length)) ** 2
    return mats, wave


def two_parts(mats):
    top = np.asarray(mats, np.float32).astype(jnp.bfloat16)
    rest = (np.asarray(mats, np.float64) - top.astype(np.float64)).astype(jnp.bfloat16)
    return top, rest


def split(x):
    top = x.astype(jnp.bfloat16)
    return top, (x - top.astype(jnp.float32)).astype(jnp.bfloat16)


def dot32(a, b):
    return jnp.dot(a, b, preferred_element_type=jnp.float32)


def right(x, hi, lo):
    top, rest = split(x)
    return dot32(top, hi) + (dot32(rest, hi) + dot32(top, lo))


def left(hi, lo, x):
    top, rest = split(x)
    return dot32(hi, top) + (dot32(lo, top) + dot32(hi, rest))


def pairs(spec):
    ends = len(spec) - 1
    return [spec[k] for k in range(1, ends)] + [(spec[0][0], spec[ends][0])]


def unpairs(groups):
    return [(groups[-1][0], None)] + groups[:-1] + [(groups[-1][1], None)]


MESH = pl.DeviceIdType.MESH
CUTS = 4


def y_forward(lines, v, rows, mats, spec):
    wide, width = lines.shape[-1], spec.shape[-1]
    inner = lines.shape[1] * wide // OUTER
    per = wide // inner
    xs = [lines[v, a // per, rows, (a % per) * inner : (a % per + 1) * inner] for a in range(OUTER)]
    each = 2 * inner // width
    for g, (re, im) in enumerate(pairs(half_spectrum(xs))):
        res = right(jnp.concatenate([re, im], axis=1), mats[0, g], mats[1, g])
        for c in range(each):
            spec[v, g * each + c, rows] = res[:, c * width : (c + 1) * width]


def y_inverse(backs, v, rows, mats, lines):
    wide, width = lines.shape[-1], backs.shape[-1]
    inner = lines.shape[1] * wide // OUTER
    per = wide // inner
    each = 2 * inner // width
    groups = []
    for g in range(OUTER // 2):
        spec = jnp.concatenate([backs[v, g * each + c, rows] for c in range(each)], axis=1)
        res = right(spec, mats[2, g], mats[3, g])
        groups.append((res[:, :inner], res[:, inner:]))
    for a, slab in enumerate(half_spectrum_t(unpairs(groups))):
        lines[v, a // per, rows, (a % per) * inner : (a % per + 1) * inner] = slab


def x_apply(full, v, ky, kx_ref, mats, out):
    count, rows, width = full.shape[1:]
    inner = count * rows // OUTER
    per = inner // rows
    slabs = [full[v, a * per : (a + 1) * per].reshape(inner, width) for a in range(OUTER)]
    groups = []
    for g, (re, im) in enumerate(pairs(half_spectrum(slabs))):
        spec = left(mats[2, g], mats[3, g], jnp.concatenate([re, im], axis=0))
        wave = kx_ref[g] + ky
        res = left(mats[0, g], mats[1, g], PRIOR_GAIN * wave * wave * spec)
        groups.append((res[:inner], res[inner:]))
    for a, res in enumerate(half_spectrum_t(unpairs(groups))):
        out[v, a * per : (a + 1) * per] = res.reshape(per, rows, width)


def settle(ref, sem):
    pltpu.make_async_copy(ref, ref, sem).wait()


def prior_kernel(
    q_ref, fhi_ref, flo_ref, thi_ref, tlo_ref, ky_ref, kx_ref, out_ref,
    lines, spec, full, backs, last, mats,
    mat_sem, own_sem, out_sem, send_lines, get_lines, send_full, get_full,
    send_backs, get_backs, send_last, get_last,
):
    across, along = lax.axis_size("gx"), lax.axis_size("gy")
    gx, gy = lax.axis_index("gx"), lax.axis_index("gy")
    count, me = across * along, gx * along + gy
    nvec, bx, by = q_ref.shape
    tall = bx // along
    step = tall // CUTS
    chunks = nvec * CUTS

    def where(p):
        return (lax.div(p, along), lax.rem(p, along))

    def span(c):
        return lax.div(c, CUTS), pl.multiple_of(lax.rem(c, CUTS) * step, step)

    def each(total, body):
        def run(i, carry):
            body(i)
            return carry

        lax.fori_loop(0, total, run, 0)

    barrier = pltpu.get_barrier_semaphore()

    def greet(i):
        p = lax.rem(me + 1 + i, count)
        pl.semaphore_signal(barrier, inc=1, device_id=where(p), device_id_type=MESH)

    each(count - 1, greet)
    pl.semaphore_wait(barrier, count - 1)

    def own_lines(v):
        return pltpu.make_async_copy(
            q_ref.at[v, pl.ds(pl.multiple_of(gy * tall, tall), tall)], lines.at[v, gy],
            own_sem.at[v],
        )

    def start_lines(c):
        v, first = span(c)

        def one(i):
            p = lax.rem(gy + 1 + i, along)
            pltpu.make_async_remote_copy(
                q_ref.at[v, pl.ds(pl.multiple_of(p * tall + first, step), step)],
                lines.at[v, gy, pl.ds(first, step)],
                send_lines.at[c], get_lines.at[c],
                device_id=(gx, p), device_id_type=MESH,
            ).start()

        each(along - 1, one)

    each(nvec, lambda v: own_lines(v).start())
    each(chunks, start_lines)
    loads = [
        pltpu.make_async_copy(ref, mats.at[i], mat_sem.at[i])
        for i, ref in enumerate((fhi_ref, flo_ref, thi_ref, tlo_ref))
    ]
    for load in loads:
        load.start()
    for load in loads[:2]:
        load.wait()
    each(nvec, lambda v: own_lines(v).wait())

    def scatter(src, dst, v, first, send, get):
        rows = pl.ds(first, step)
        dst[v, me, rows] = src[v, me, rows]

        def one(i):
            p = lax.rem(me + 1 + i, count)
            pltpu.make_async_remote_copy(
                src.at[v, p, rows], dst.at[v, me, rows], send, get,
                device_id=where(p), device_id_type=MESH,
            ).start()

        each(count - 1, one)

    def forward_y(c):
        v, first = span(c)
        rows = pl.ds(first, step)
        settle(lines.at[v, pl.ds(0, along - 1), rows], get_lines.at[c])
        y_forward(lines, v, rows, mats, spec)
        scatter(spec, full, v, first, send_full.at[v], get_full.at[v])

    each(chunks, forward_y)
    for load in loads[2:]:
        load.wait()

    def along_x(v):
        settle(full.at[v, pl.ds(0, count - 1)], get_full.at[v])
        settle(spec.at[v, pl.ds(0, count - 1)], send_full.at[v])
        x_apply(full, v, ky_ref[pl.ds(me, 1)], kx_ref, mats, spec)

        def part(h):
            c = v * CUTS + h
            first = pl.multiple_of(h * step, step)
            scatter(spec, backs, v, first, send_backs.at[c], get_backs.at[c])

        each(CUTS, part)

    each(nvec, along_x)

    def out_copy(c, s):
        v, first = span(c)
        rows = pl.ds(pl.multiple_of(s * tall + first, step), step)
        return pltpu.make_async_copy(last.at[v, s, pl.ds(first, step)], out_ref.at[v, rows], out_sem.at[c, s])

    def finish(c):
        v, first = span(c)
        settle(last.at[v, pl.ds(0, along - 1), pl.ds(first, step)], get_last.at[c])
        each(along, lambda s: out_copy(c, s).start())

    def backward_y(c):
        v, first = span(c)
        rows = pl.ds(first, step)
        settle(backs.at[v, pl.ds(0, count - 1), rows], get_backs.at[c])
        y_inverse(backs, v, rows, mats, lines)
        last[v, gy, rows] = lines[v, gy, rows]

        def one(i):
            p = lax.rem(gy + 1 + i, along)
            pltpu.make_async_remote_copy(
                lines.at[v, p, rows], last.at[v, gy, rows], send_last.at[c], get_last.at[c],
                device_id=(gx, p), device_id_type=MESH,
            ).start()

        each(along - 1, one)

        @pl.when(c > 0)
        def _():
            finish(c - 1)

    each(chunks, backward_y)
    finish(chunks - 1)

    def drain(c):
        v, first = span(c)
        rows = pl.ds(first, step)
        settle(lines.at[v, pl.ds(0, along - 1), rows], send_lines.at[c])
        settle(lines.at[v, pl.ds(0, along - 1), rows], send_last.at[c])
        settle(spec.at[v, pl.ds(0, count - 1), rows], send_backs.at[c])
        each(along, lambda s: out_copy(c, s).wait())

    each(chunks, drain)


def cost(flops, moved):
    return pl.CostEstimate(flops=int(flops), bytes_accessed=int(moved), transcendentals=0)


def prior(q):
    across, along = lax.axis_size("gx"), lax.axis_size("gy")
    nvec, bx, by = q.shape
    length = by * along
    count = across * along
    rows = bx // along
    width = length // count
    mats, wave = line_tables(length)
    fhi, flo = two_parts(mats)
    thi, tlo = two_parts(np.swapaxes(mats, 1, 2))
    ky = jnp.asarray(wave.reshape(count, width), jnp.float32)
    kx = jnp.asarray(wave[:, :, None], jnp.float32)
    lines = pltpu.VMEM((nvec, along, rows, by), jnp.float32)
    packed = pltpu.VMEM((nvec, count, rows, width), jnp.float32)
    chunks = nvec * CUTS
    dma = pltpu.SemaphoreType.DMA
    anywhere, inside = pl.BlockSpec(memory_space=pl.ANY), pl.BlockSpec(memory_space=pltpu.VMEM)
    return pl.pallas_call(
        prior_kernel,
        in_specs=[anywhere] * 5 + [inside] * 2,
        out_specs=anywhere,
        out_shape=jax.ShapeDtypeStruct(q.shape, jnp.float32),
        scratch_shapes=[
            lines, packed, packed, packed, lines, pltpu.VMEM((4,) + mats.shape, jnp.bfloat16),
            dma((4,)), dma((nvec,)), dma((chunks, along)), dma((chunks,)), dma((chunks,)),
            dma((nvec,)), dma((nvec,)), dma((chunks,)), dma((chunks,)), dma((chunks,)),
            dma((chunks,)),
        ],
        compiler_params=pltpu.CompilerParams(
            vmem_limit_bytes=VMEM_BYTES, collective_id=0, has_side_effects=True
        ),
        cost_estimate=cost(36 * mats.size * nvec * bx * by // length, 64 * nvec * bx * by),
        name="prior",
    )(q, fhi, flo, thi, tlo, ky, kx)


RIM = 8
VMEM_BYTES = 58 * 2**20


def shift(axis, step):
    count = lax.axis_size(axis)
    return [(i, i + step) for i in range(count) if 0 <= i + step < count]


def near(q, heat, labels, cut):
    first = cut(q)
    return jnp.concatenate(
        [
            first,
            (cut(labels) + 1).astype(jnp.float32).reshape((-1,) + first.shape[1:]),
            cut(heat).reshape((-1,) + first.shape[1:])[:-1],
        ]
    )


def rim_rows(q, heat, labels):
    bx = q.shape[1]
    above = lax.ppermute(
        near(q, heat, labels, lambda f: f[..., bx - RIM :, :]), "gx", shift("gx", 1)
    )
    below = lax.ppermute(near(q, heat, labels, lambda f: f[..., :RIM, :]), "gx", shift("gx", -1))
    return above, below


def rim_sides(q, heat, labels, above, below):
    by = q.shape[2]
    ends = []
    for cols, step in ((slice(0, RIM), -1), (slice(by - RIM, by), 1)):
        line = jnp.concatenate(
            [above[..., cols], near(q, heat, labels, lambda f: f[..., cols]), below[..., cols]],
            axis=1,
        )
        ends.append(lax.ppermute(jnp.swapaxes(line, 1, 2), "gy", shift("gy", step)))
    gap = jnp.zeros((ends[0].shape[0], 128 - 2 * RIM, ends[0].shape[2]), jnp.float32)
    return jnp.swapaxes(jnp.concatenate([ends[0], gap, ends[1]], axis=1), 1, 2)


def data_strips(q_ref, heat_ref, labels_ref, above_ref, below_ref, side_ref, out_ref, f_ref):
    nvec, bx, by = out_ref.shape
    f_ref[:, :RIM, :by] = above_ref[...]
    f_ref[:, RIM + bx :, :by] = below_ref[...]
    f_ref[:, :, by:] = side_ref[...]
    levels_at = nvec + 4
    for v in range(nvec):
        f_ref[v, RIM : RIM + bx, :by] = q_ref[v]
    for i in range(4):
        f_ref[nvec + i, RIM : RIM + bx, :by] = (labels_ref[i // 2, i % 2] + 1).astype(jnp.float32)
    for i in range(3):
        f_ref[levels_at + i, RIM : RIM + bx, :by] = heat_ref[i]
    strip = 32
    tall, wide = strip + 2 * RIM, f_ref.shape[2]

    def rim(f):
        return (pltpu.roll(f, 1, 0) + pltpu.roll(f, tall - 1, 0)) + (
            pltpu.roll(f, 1, 1) + pltpu.roll(f, wide - 1, 1)
        )

    def one(s, carry):
        first = pl.multiple_of(s * strip, strip)
        field = lambda i: f_ref[i, pl.ds(first, tall), :]

        def inverse_capacity(label):
            return jnp.where(label == 2.0, 0.25, jnp.where(label == 3.0, 0.8, 1.0))

        def conduct(label, level):
            base = jnp.where(
                label == 1.0, 1.0, jnp.where(label == 2.0, 0.6, jnp.where(label == 3.0, 0.35, 0.0))
            )
            return TIME_STEP * base * (1.0 + 0.5 * jnp.tanh(level))

        label = [field(nvec + i) for i in range(4)]
        ic_top0, ic_top1 = inverse_capacity(label[0]), inverse_capacity(label[2])
        ic_low1 = inverse_capacity(label[3])
        c_top0 = conduct(label[0], field(nvec + 4))
        c_low0 = conduct(label[1], field(nvec + 5))
        c_top1 = conduct(label[2], field(nvec + 6))
        for v in range(nvec):
            q = field(v)
            first_u = TIME_STEP * q * ic_top0
            second_top = (2.0 * TIME_STEP) * q + c_top0 * (rim(first_u) - 6.0 * first_u)
            top_u = second_top * ic_top1
            low_u = c_low0 * first_u * ic_low1
            third_top = (
                second_top + c_top1 * (rim(top_u) - 6.0 * top_u + low_u) + TIME_STEP * q
            )
            adj_three = OBS_WEIGHT * third_top * ic_top1 * ic_top1
            push_top = c_top1 * adj_three
            adj_two = adj_three + (rim(push_top) - 6.0 * push_top) * ic_top1
            pull_top = c_top0 * adj_two
            pull_low = c_low0 * (push_top * ic_low1)
            adj_one = adj_two + (rim(pull_top) - 6.0 * pull_top + pull_low) * ic_top0
            total = TIME_STEP * (adj_three + adj_two + adj_one)
            out_ref[v, pl.ds(first, strip), :] = total[RIM : RIM + strip, :by]
        return carry

    lax.fori_loop(0, bx // strip, one, 0)


def data_part(q, heat, labels, above, below, side):
    nvec, bx, by = q.shape
    levels = heat.reshape(-1, bx, by)
    whole = lambda x: pl.BlockSpec(x.shape, lambda i: (0,) * x.ndim)
    return pl.pallas_call(
        data_strips,
        grid=(1,),
        in_specs=[
            whole(q), pl.BlockSpec((3, bx, by), lambda i: (0, 0, 0)), whole(labels),
            whole(above), whole(below), whole(side),
        ],
        out_specs=whole(q),
        out_shape=jax.ShapeDtypeStruct(q.shape, jnp.float32),
        scratch_shapes=[pltpu.VMEM((nvec + 7, bx + 2 * RIM, by + 128), jnp.float32)],
        compiler_params=pltpu.CompilerParams(vmem_limit_bytes=VMEM_BYTES),
        cost_estimate=cost(400 * q.size, 24 * q.size),
        name="data_strips",
    )(q, levels, labels, above, below, side)


def shards(q, heat, labels):
    nvec, bx, by = q.shape
    along, across = lax.axis_size("gy"), lax.axis_size("gx")
    rows, width = bx // along, by // across
    square = bx * across == by * along
    if not square or rows % 16 or width % 128 or by % (by * along // OUTER) or bx % 32:
        return shards_general(q, heat, labels)
    above, below = rim_rows(q, heat, labels)
    side = rim_sides(q, heat, labels, above, below)
    return data_part(q, heat, labels, above, below, side) + prior(q)


def solution(mesh):
    in_specs = (P(None, "gx", "gy"), P(None, None, "gx", "gy"), P(None, None, "gx", "gy"))
    out_specs = P(None, "gx", "gy")
    return jax.shard_map(shards, mesh=mesh, in_specs=in_specs, out_specs=out_specs, check_vma=False)
```

```python
import math

import jax
import jax.numpy as jnp
import numpy as np
from jax import lax
from jax.experimental import pallas as pl
from jax.experimental.pallas import tpu as pltpu
from jax.sharding import PartitionSpec as P

TIME_STEP = 0.1
OBS_WEIGHT = 10.0
PRIOR_GAIN = 0.005
HIGHEST = lax.Precision.HIGHEST


def with_halo(cells, sides, width):
    for axis, dim in sides:
        count = lax.axis_size(axis)
        ends = count - 1
        head = lax.slice_in_dim(cells, 0, width, axis=dim)
        tail = lax.slice_in_dim(cells, cells.shape[dim] - width, cells.shape[dim], axis=dim)
        cells = jnp.concatenate(
            [
                lax.ppermute(tail, axis, [(i, (i + 1) % count) for i in range(ends)]),
                cells,
                lax.ppermute(head, axis, [((i + 1) % count, i) for i in range(ends)]),
            ],
            axis=dim,
        )
    return cells


def surface_rim(field):
    padded = with_halo(field, (("gx", 1), ("gy", 2)), 1)
    return padded[:, 2:, 1:-1] + padded[:, :-2, 1:-1] + padded[:, 1:-1, 2:] + padded[:, 1:-1, :-2]


def cos_sin(horizontal_line_total, col_count, modulus):
    row_ids = jnp.arange(horizontal_line_total, dtype=jnp.int32)[:, None]
    col_ids = jnp.arange(col_count, dtype=jnp.int32)[None, :]
    angles = (row_ids * col_ids % modulus).astype(jnp.float32) * (2.0 * math.pi / modulus)
    return (jnp.cos(angles), jnp.sin(angles))


def tables(length):
    bit_count = length.bit_length() - 1
    outer_len = 2 ** (bit_count // 2)
    inner_len = length // outer_len
    cos_outer, sin_outer = cos_sin(outer_len, outer_len, outer_len)
    cos_inner, sin_inner = cos_sin(inner_len, inner_len, inner_len)
    twist_cos, twist_sin = cos_sin(outer_len, inner_len, length)
    outer_fwd = jnp.stack([cos_outer, -sin_outer])
    inner_fwd = jnp.stack([jnp.stack([cos_inner, -sin_inner]), jnp.stack([sin_inner, cos_inner])])
    inner_inv = jnp.stack([jnp.stack([cos_inner, sin_inner]), jnp.stack([-sin_inner, cos_inner])])
    outer_inv = jnp.stack([cos_outer, -sin_outer])
    freq_index = (
        jnp.arange(outer_len, dtype=jnp.int32)[:, None]
        + outer_len * jnp.arange(inner_len, dtype=jnp.int32)[None, :]
    )
    signed = jnp.where(freq_index < length // 2, freq_index, freq_index - length).astype(
        jnp.float32
    )
    wave_sq = (signed * (2.0 * math.pi / length)) ** 2
    return (
        length,
        outer_len,
        inner_len,
        outer_fwd,
        inner_fwd,
        inner_inv,
        outer_inv,
        twist_cos,
        twist_sin,
        wave_sq,
    )


def forward(field, table):
    (
        length,
        outer_len,
        inner_len,
        outer_fwd,
        inner_fwd,
        inner_inv,
        outer_inv,
        twist_cos,
        twist_sin,
        wave_sq,
    ) = table
    grid = field.reshape(field.shape[:-1] + (outer_len, inner_len))
    stepped = jnp.einsum("...ab,rak->...rkb", grid, outer_fwd, precision=HIGHEST)
    step_re = stepped[..., 0, :, :]
    step_im = stepped[..., 1, :, :]
    twisted = jnp.stack(
        [step_re * twist_cos + step_im * twist_sin, step_im * twist_cos - step_re * twist_sin],
        axis=-3,
    )
    spec = jnp.einsum("...rkb,rsbm->...skm", twisted, inner_fwd, precision=HIGHEST)
    return (spec[..., 0, :, :], spec[..., 1, :, :])


def inverse(spec_re, spec_im, table):
    (
        length,
        outer_len,
        inner_len,
        outer_fwd,
        inner_fwd,
        inner_inv,
        outer_inv,
        twist_cos,
        twist_sin,
        wave_sq,
    ) = table
    stacked = jnp.stack([spec_re, spec_im], axis=-3)
    halved = jnp.einsum("...skm,srbm->...rkb", stacked, inner_inv, precision=HIGHEST)
    half_re = halved[..., 0, :, :]
    half_im = halved[..., 1, :, :]
    turned = jnp.stack(
        [half_re * twist_cos - half_im * twist_sin, half_im * twist_cos + half_re * twist_sin],
        axis=-3,
    )
    grid = jnp.einsum("...rkb,rka->...ab", turned, outer_inv, precision=HIGHEST)
    return grid.reshape(grid.shape[:-2] + (length,)) / length


def shards_general(flux_perturbation, archived_nominal_heat_levels, archived_solidity_labels):
    capacity = jnp.where(
        archived_solidity_labels == 0, 1.0, jnp.where(archived_solidity_labels == 1, 4.0, 1.25)
    ).astype(jnp.float32)
    diffusion_advance = jnp.where(
        archived_solidity_labels == 0, 1.0, jnp.where(archived_solidity_labels == 1, 0.6, 0.35)
    ).astype(jnp.float32)
    diffusion_advance = diffusion_advance * (1.0 + 0.5 * jnp.tanh(archived_nominal_heat_levels))
    rows = lax.all_to_all(flux_perturbation, "gx", split_axis=2, concat_axis=1, tiled=True)
    row_table = tables(rows.shape[1])
    first_u = TIME_STEP * flux_perturbation / capacity[0, 0]
    second_top = TIME_STEP * flux_perturbation + TIME_STEP * (
        diffusion_advance[0, 0] * (surface_rim(first_u) - 6.0 * first_u) + flux_perturbation
    )
    second_low = TIME_STEP * diffusion_advance[0, 1] * first_u
    top_u = second_top / capacity[1, 0]
    low_u = second_low / capacity[1, 1]
    third_top = second_top + TIME_STEP * (
        diffusion_advance[1, 0] * (surface_rim(top_u) - 6.0 * top_u + low_u) + flux_perturbation
    )
    misfit = OBS_WEIGHT * third_top / capacity[1, 0]
    adj_three = misfit / capacity[1, 0]
    push_top = TIME_STEP * diffusion_advance[1, 0] * adj_three
    adj_two_top = adj_three + (surface_rim(push_top) - 6.0 * push_top) / capacity[1, 0]
    adj_two_low = push_top / capacity[1, 1]
    pull_top = TIME_STEP * diffusion_advance[0, 0] * adj_two_top
    pull_low = TIME_STEP * diffusion_advance[0, 1] * adj_two_low
    adj_one_top = adj_two_top + (surface_rim(pull_top) - 6.0 * pull_top + pull_low) / capacity[0, 0]
    data_term = TIME_STEP * (adj_three + adj_two_top + adj_one_top)
    row_re, row_im = forward(jnp.swapaxes(rows, 1, 2), row_table)
    wave_x = row_table[-1]
    second_x = jnp.swapaxes(
        inverse(2.0 * PRIOR_GAIN * wave_x * row_re, 2.0 * PRIOR_GAIN * wave_x * row_im, row_table),
        1,
        2,
    )
    fourth_x = jnp.swapaxes(
        inverse(
            PRIOR_GAIN * wave_x * wave_x * row_re, PRIOR_GAIN * wave_x * wave_x * row_im, row_table
        ),
        1,
        2,
    )
    second_back, fourth_part = (
        lax.all_to_all(second_x, "gx", split_axis=1, concat_axis=2, tiled=True),
        lax.all_to_all(fourth_x, "gx", split_axis=1, concat_axis=2, tiled=True),
    )
    cols_dir, cols_second = (
        lax.all_to_all(flux_perturbation, "gy", split_axis=1, concat_axis=2, tiled=True),
        lax.all_to_all(second_back, "gy", split_axis=1, concat_axis=2, tiled=True),
    )
    col_table = tables(cols_dir.shape[2])
    dir_re, dir_im = forward(cols_dir, col_table)
    sec_re, sec_im = forward(cols_second, col_table)
    wave_y = col_table[-1]
    mixed = inverse(
        PRIOR_GAIN * wave_y * wave_y * dir_re + wave_y * sec_re,
        PRIOR_GAIN * wave_y * wave_y * dir_im + wave_y * sec_im,
        col_table,
    )
    mixed_back = lax.all_to_all(mixed, "gy", split_axis=2, concat_axis=1, tiled=True)
    return data_term + fourth_part + mixed_back


OUTER = 16


def half_spectrum(xs):
    n = len(xs)
    if n == 2:
        return [(xs[0] + xs[1], None), (xs[0] - xs[1], None)]
    even, odd = half_spectrum(xs[0::2]), half_spectrum(xs[1::2])
    out = [None] * (n // 2 + 1)
    for k in range(n // 4 + 1):
        er, ei = even[k]
        orr, oi = odd[k]
        if k == 0:
            out[0] = (er + orr, None)
            out[n // 2] = (er - orr, None)
        elif k == n // 4:
            out[k] = (er, -orr)
        else:
            c, s = math.cos(2 * math.pi * k / n), math.sin(2 * math.pi * k / n)
            if 8 * k == n:
                tr, ti = c * (orr + oi), c * (oi - orr)
            else:
                tr, ti = c * orr + s * oi, c * oi - s * orr
            out[k] = (er + tr, ei + ti)
            out[n // 2 - k] = (er - tr, ti - ei)
    return out


def half_spectrum_t(gs):
    half = len(gs) - 1
    n = 2 * half
    if n == 2:
        return [gs[0][0] + gs[1][0], gs[0][0] - gs[1][0]]
    even, odd = [], []
    for m in range(n // 4 + 1):
        gr, gi = gs[m]
        if m == 0:
            hr = gs[half][0]
            even.append((gr + hr, None))
            odd.append((gr - hr, None))
        elif m == n // 4:
            even.append((gr, None))
            odd.append((-gi, None))
        else:
            hr, hi = gs[half - m]
            even.append((gr + hr, gi - hi))
            dr, di = gr - hr, gi + hi
            c, s = math.cos(2 * math.pi * m / n), math.sin(2 * math.pi * m / n)
            if 8 * m == n:
                odd.append((c * (dr - di), c * (dr + di)))
            else:
                odd.append((c * dr - s * di, c * di + s * dr))
    out = [None] * n
    out[0::2] = half_spectrum_t(even)
    out[1::2] = half_spectrum_t(odd)
    return out


def line_tables(length):
    inner = length // OUTER
    groups = OUTER // 2
    b = np.arange(inner)[:, None]
    mats = np.zeros((groups, 2 * inner, 2 * inner))
    freq = np.zeros((groups, 2 * inner), np.int64)
    scale = math.sqrt(2.0 / length)
    for k1 in range(1, groups):
        k = k1 + OUTER * np.arange(inner)
        angle = 2.0 * math.pi * ((b * k[None, :]) % length) / length
        c, s = np.cos(angle) * scale, np.sin(angle) * scale
        mats[k1 - 1] = np.block([[c, -s], [s, c]])
        freq[k1 - 1] = np.concatenate([k, k])
    last = groups - 1
    for part, first in ((0, 0), (1, groups)):
        k = first + OUTER * np.arange(inner // 2)
        angle = 2.0 * math.pi * ((b * k[None, :]) % length) / length
        c, s = np.cos(angle) * scale, np.sin(angle) * scale
        k_sin = k.copy()
        if first == 0:
            c[:, 0] = math.sqrt(1.0 / length)
            k_sin[0] = length // 2
            s[:, 0] = -math.sqrt(1.0 / length) * (1 - 2 * (np.arange(inner) % 2))
        span = slice(part * inner, (part + 1) * inner)
        mats[last][span, span] = np.concatenate([c, -s], axis=1)
        freq[last][span] = np.concatenate([k, k_sin])
    signed = np.where(freq < length // 2, freq, freq - length)
    wave = (signed * (2.0 * math.pi / length)) ** 2
    return mats, wave


def two_parts(mats):
    top = np.asarray(mats, np.float32).astype(jnp.bfloat16)
    rest = (np.asarray(mats, np.float64) - top.astype(np.float64)).astype(jnp.bfloat16)
    return top, rest


def split(x):
    top = x.astype(jnp.bfloat16)
    return top, (x - top.astype(jnp.float32)).astype(jnp.bfloat16)


def dot32(a, b):
    return jnp.dot(a, b, preferred_element_type=jnp.float32)


def right(x, hi, lo):
    top, rest = split(x)
    return dot32(top, hi) + (dot32(rest, hi) + dot32(top, lo))


def left(hi, lo, x):
    top, rest = split(x)
    return dot32(hi, top) + (dot32(lo, top) + dot32(hi, rest))


def pairs(spec):
    ends = len(spec) - 1
    return [spec[k] for k in range(1, ends)] + [(spec[0][0], spec[ends][0])]


def unpairs(groups):
    return [(groups[-1][0], None)] + groups[:-1] + [(groups[-1][1], None)]


MESH = pl.DeviceIdType.MESH
CUTS = 4


def y_forward(lines, v, rows, mats, spec):
    wide, width = lines.shape[-1], spec.shape[-1]
    inner = lines.shape[1] * wide // OUTER
    per = wide // inner
    xs = [lines[v, a // per, rows, (a % per) * inner : (a % per + 1) * inner] for a in range(OUTER)]
    each = 2 * inner // width
    for g, (re, im) in enumerate(pairs(half_spectrum(xs))):
        res = right(jnp.concatenate([re, im], axis=1), mats[0, g], mats[1, g])
        for c in range(each):
            spec[v, g * each + c, rows] = res[:, c * width : (c + 1) * width]


def y_inverse(backs, v, rows, mats, lines):
    wide, width = lines.shape[-1], backs.shape[-1]
    inner = lines.shape[1] * wide // OUTER
    per = wide // inner
    each = 2 * inner // width
    groups = []
    for g in range(OUTER // 2):
        spec = jnp.concatenate([backs[v, g * each + c, rows] for c in range(each)], axis=1)
        res = right(spec, mats[2, g], mats[3, g])
        groups.append((res[:, :inner], res[:, inner:]))
    for a, slab in enumerate(half_spectrum_t(unpairs(groups))):
        lines[v, a // per, rows, (a % per) * inner : (a % per + 1) * inner] = slab


def x_apply(full, v, ky, kx_ref, mats, out):
    count, rows, width = full.shape[1:]
    inner = count * rows // OUTER
    per = inner // rows
    slabs = [full[v, a * per : (a + 1) * per].reshape(inner, width) for a in range(OUTER)]
    groups = []
    for g, (re, im) in enumerate(pairs(half_spectrum(slabs))):
        spec = left(mats[2, g], mats[3, g], jnp.concatenate([re, im], axis=0))
        wave = kx_ref[g] + ky
        res = left(mats[0, g], mats[1, g], PRIOR_GAIN * wave * wave * spec)
        groups.append((res[:inner], res[inner:]))
    for a, res in enumerate(half_spectrum_t(unpairs(groups))):
        out[v, a * per : (a + 1) * per] = res.reshape(per, rows, width)


def settle(ref, sem):
    pltpu.make_async_copy(ref, ref, sem).wait()


def whole_kernel(
    q_ref, heat_ref, labels_ref, fhi_ref, flo_ref, thi_ref, tlo_ref, ky_ref, kx_ref, out_ref,
    lines, spec, full, backs, last, mats, data, ends, edges, packs, strips,
    mat_sem, own_sem, out_sem, send_lines, get_lines, send_full, get_full,
    send_backs, get_backs, send_last, get_last,
    send_ends, get_ends, edge_sem, send_packs, get_packs, strip_sem,
):
    across, along = lax.axis_size("gx"), lax.axis_size("gy")
    gx, gy = lax.axis_index("gx"), lax.axis_index("gy")
    count, me = across * along, gx * along + gy
    nvec, bx, by = q_ref.shape
    tall = bx // along
    step = tall // CUTS
    chunks = nvec * CUTS

    def where(p):
        return (lax.div(p, along), lax.rem(p, along))

    def span(c):
        return lax.div(c, CUTS), pl.multiple_of(lax.rem(c, CUTS) * step, step)

    def each(total, body):
        def run(i, carry):
            body(i)
            return carry

        lax.fori_loop(0, total, run, 0)

    barrier = pltpu.get_barrier_semaphore()

    def greet(i):
        p = lax.rem(me + 1 + i, count)
        pl.semaphore_signal(barrier, inc=1, device_id=where(p), device_id_type=MESH)

    each(count - 1, greet)
    pl.semaphore_wait(barrier, count - 1)

    def own_lines(v):
        return pltpu.make_async_copy(
            q_ref.at[v, pl.ds(pl.multiple_of(gy * tall, tall), tall)], lines.at[v, gy],
            own_sem.at[v],
        )

    def start_lines(c):
        v, first = span(c)

        def one(i):
            p = lax.rem(gy + 1 + i, along)
            pltpu.make_async_remote_copy(
                q_ref.at[v, pl.ds(pl.multiple_of(p * tall + first, step), step)],
                lines.at[v, gy, pl.ds(first, step)],
                send_lines.at[c], get_lines.at[c],
                device_id=(gx, p), device_id_type=MESH,
            ).start()

        each(along - 1, one)

    each(nvec, lambda v: own_lines(v).start())
    start_lines(0)
    sources = (q_ref, heat_ref, labels_ref)

    def end_copy(side, kind, target):
        src, dst = sources[kind], ends[kind]
        first = bx - RIM if side == 0 else 0
        return pltpu.make_async_remote_copy(
            src.at[pl.ds(0, dst.shape[1]), pl.ds(first, RIM)], dst.at[side],
            send_ends.at[side, kind], get_ends.at[side, kind],
            device_id=(target, gy), device_id_type=MESH,
        )

    def edge_copy(side, kind):
        src, dst = sources[kind], edges[kind]
        return pltpu.make_async_copy(
            src.at[pl.ds(0, dst.shape[1]), :, pl.ds(by - 128 if side else 0, 128)], dst.at[side],
            edge_sem.at[side, kind],
        )

    for side, (sends, target) in enumerate(((gx < across - 1, gx + 1), (gx > 0, gx - 1))):

        @pl.when(sends)
        def _():
            for kind in range(3):
                end_copy(side, kind, target).start()

        @pl.when(gx == (0 if side == 0 else across - 1))
        def _():
            for kind in range(3):
                ref = ends[kind]
                ref[side] = jnp.full(ref.shape[1:], -1 if kind == 2 else 0, ref.dtype)

        @pl.when(gy == (along - 1 if side == 0 else 0))
        def _():
            packs[2 + side] = jnp.zeros(packs.shape[1:], jnp.float32)

    loads = [
        pltpu.make_async_copy(ref, mats.at[i], mat_sem.at[i])
        for i, ref in enumerate((fhi_ref, flo_ref, thi_ref, tlo_ref))
    ]
    for load in loads:
        load.start()
    each(chunks - 1, lambda c: start_lines(c + 1))
    for side in range(2):
        for kind in range(3):
            edge_copy(side, kind).start()
    for load in loads[:2]:
        load.wait()
    each(nvec, lambda v: own_lines(v).wait())

    def scatter(src, dst, v, first, send, get):
        rows = pl.ds(first, step)
        dst[v, me, rows] = src[v, me, rows]

        def one(i):
            p = lax.rem(me + 1 + i, count)
            pltpu.make_async_remote_copy(
                src.at[v, p, rows], dst.at[v, me, rows], send, get,
                device_id=where(p), device_id_type=MESH,
            ).start()

        each(count - 1, one)

    def forward_y(c):
        v, first = span(c)
        rows = pl.ds(first, step)
        settle(lines.at[v, pl.ds(0, along - 1), rows], get_lines.at[c])
        y_forward(lines, v, rows, mats, spec)
        scatter(spec, full, v, first, send_full.at[v], get_full.at[v])

    each(CUTS, forward_y)

    def packed(side, fields):
        lane = lax.broadcasted_iota(jnp.int32, fields[0].shape, 1)
        total = jnp.zeros(fields[0].shape, jnp.float32)
        for i, f in enumerate(fields):
            moved = pltpu.roll(f, RIM * (i + side), 1)
            total = jnp.where((lane >= RIM * i) & (lane < RIM * (i + 1)), moved, total)
        return total

    def nine(q, level, label):
        return (
            [q(v) for v in range(nvec)]
            + [(label(i) + 1).astype(jnp.float32) for i in range(4)]
            + [level(i) for i in range(3)]
        )

    for side, gets in enumerate((gx > 0, gx < across - 1)):

        @pl.when(gets)
        def _():
            for kind in range(3):
                settle(ends[kind].at[side], get_ends.at[side, kind])

    for side in range(2):
        for kind in range(3):
            edge_copy(side, kind).wait()
        cols = slice(by - 128, by) if side else slice(0, 128)
        for end, at in ((0, 0), (1, RIM + bx)):
            packs[side, at : at + RIM] = packed(
                side, nine(*[lambda i, r=r: r[end, i, :, cols] for r in ends])
            )

        def pack_some(n):
            first = pl.multiple_of(n * 64, 64)
            packs[side, pl.ds(pl.multiple_of(first + RIM, RIM), 64)] = packed(
                side, nine(*[lambda i, r=r: r[side, i, pl.ds(first, 64)] for r in edges])
            )

        each(bx // 64, pack_some)

    def pack_copy(side, target):
        return pltpu.make_async_remote_copy(
            packs.at[side], packs.at[2 + side], send_packs.at[side], get_packs.at[side],
            device_id=(gx, target), device_id_type=MESH,
        )

    for side, (sends, target) in enumerate(((gy > 0, gy - 1), (gy < along - 1, gy + 1))):

        @pl.when(sends)
        def _():
            pack_copy(side, target).start()

    total = bx // STRIP
    strip_tall = STRIP + 2 * RIM

    def strip_copy(s, slot):
        for kind in range(3):
            src, dst, sem = sources[kind], strips[kind], strip_sem.at[slot, kind]
            depth = pl.ds(0, dst.shape[1])

            @pl.when((s > 0) & (s < total - 1))
            def _():
                rows = pl.ds(pl.multiple_of(s * STRIP - RIM, RIM), strip_tall)
                pltpu.make_async_copy(src.at[depth, rows], dst.at[slot], sem).start()

            for edge, side, near_at, far_at, from_at in (
                (0, 0, 0, RIM, 0),
                (total - 1, 1, STRIP + RIM, 0, bx - STRIP - RIM),
            ):

                @pl.when(s == edge)
                def _():
                    pltpu.make_async_copy(
                        ends[kind].at[side], dst.at[slot, :, pl.ds(near_at, RIM)], sem
                    ).start()
                    pltpu.make_async_copy(
                        src.at[depth, pl.ds(from_at, STRIP + RIM)],
                        dst.at[slot, :, pl.ds(far_at, STRIP + RIM)],
                        sem,
                    ).start()

    def strip_work(s):
        slot = lax.rem(s, 2)
        for kind in range(3):
            settle(strips[kind].at[slot], strip_sem.at[slot, kind])

        @pl.when(s + 1 < total)
        def _():
            strip_copy(s + 1, 1 - slot)

        first = pl.multiple_of(s * STRIP, STRIP)
        over, under = (packs[side, pl.ds(first, strip_tall)] for side in (2, 3))
        lane = lax.broadcasted_iota(jnp.int32, over.shape, 1)

        def side_of(i):
            return jnp.where(
                lane < RIM,
                pltpu.roll(over, (128 - RIM * i) % 128, 1),
                jnp.where(lane >= 128 - RIM, pltpu.roll(under, 128 - RIM - RIM * i, 1), 0.0),
            )

        middle = nine(*[lambda i, r=r: r[slot, i] for r in strips])
        fields = [jnp.concatenate([f, side_of(i)], axis=1) for i, f in enumerate(middle)]
        for v, res in enumerate(data_strip(fields, nvec)):
            data[v, pl.ds(first, STRIP)] = res[RIM : RIM + STRIP, :by]

    strip_copy(jnp.int32(0), 0)
    each(chunks - CUTS, lambda c: forward_y(c + CUTS))
    for load in loads[2:]:
        load.wait()
    for side, gets in enumerate((gy < along - 1, gy > 0)):

        @pl.when(gets)
        def _():
            settle(packs.at[2 + side], get_packs.at[side])

    def along_x(v):
        each(total // nvec, lambda i: strip_work(v * (total // nvec) + i))
        settle(full.at[v, pl.ds(0, count - 1)], get_full.at[v])
        settle(spec.at[v, pl.ds(0, count - 1)], send_full.at[v])
        x_apply(full, v, ky_ref[pl.ds(me, 1)], kx_ref, mats, spec)

        def part(h):
            c = v * CUTS + h
            first = pl.multiple_of(h * step, step)
            scatter(spec, backs, v, first, send_backs.at[c], get_backs.at[c])

        each(CUTS, part)

    each(nvec, along_x)

    def out_copy(c, s):
        v, first = span(c)
        rows = pl.ds(pl.multiple_of(s * tall + first, step), step)
        return pltpu.make_async_copy(data.at[v, rows], out_ref.at[v, rows], out_sem.at[c, s])

    def finish(c):
        v, first = span(c)
        settle(last.at[v, pl.ds(0, along - 1), pl.ds(first, step)], get_last.at[c])

        def one(s):
            rows = pl.ds(pl.multiple_of(s * tall + first, step), step)
            data[v, rows] = data[v, rows] + last[v, s, pl.ds(first, step)]
            out_copy(c, s).start()

        each(along, one)

    def backward_y(c):
        v, first = span(c)
        rows = pl.ds(first, step)
        settle(backs.at[v, pl.ds(0, count - 1), rows], get_backs.at[c])
        y_inverse(backs, v, rows, mats, lines)
        last[v, gy, rows] = lines[v, gy, rows]

        def one(i):
            p = lax.rem(gy + 1 + i, along)
            pltpu.make_async_remote_copy(
                lines.at[v, p, rows], last.at[v, gy, rows], send_last.at[c], get_last.at[c],
                device_id=(gx, p), device_id_type=MESH,
            ).start()

        each(along - 1, one)

        @pl.when(c > 0)
        def _():
            finish(c - 1)

    each(chunks, backward_y)
    finish(chunks - 1)

    def drain(c):
        v, first = span(c)
        rows = pl.ds(first, step)
        settle(lines.at[v, pl.ds(0, along - 1), rows], send_lines.at[c])
        settle(lines.at[v, pl.ds(0, along - 1), rows], send_last.at[c])
        settle(spec.at[v, pl.ds(0, count - 1), rows], send_backs.at[c])
        each(along, lambda s: out_copy(c, s).wait())

    each(chunks, drain)
    for side, sends in enumerate((gx < across - 1, gx > 0)):

        @pl.when(sends)
        def _():
            for kind in range(3):
                settle(ends[kind].at[side], send_ends.at[side, kind])

    for side, sends in enumerate((gy > 0, gy < along - 1)):

        @pl.when(sends)
        def _():
            settle(packs.at[side], send_packs.at[side])


def cost(flops, moved):
    return pl.CostEstimate(flops=int(flops), bytes_accessed=int(moved), transcendentals=0)


def whole(q, heat, labels):
    across, along = lax.axis_size("gx"), lax.axis_size("gy")
    nvec, bx, by = q.shape
    length = by * along
    count = across * along
    rows = bx // along
    width = length // count
    mats, wave = line_tables(length)
    fhi, flo = two_parts(mats)
    thi, tlo = two_parts(np.swapaxes(mats, 1, 2))
    ky = jnp.asarray(wave.reshape(count, width), jnp.float32)
    kx = jnp.asarray(wave[:, :, None], jnp.float32)
    lines = pltpu.VMEM((nvec, along, rows, by), jnp.float32)
    packed = pltpu.VMEM((nvec, count, rows, width), jnp.float32)
    chunks = nvec * CUTS
    levels, labels = heat.reshape(-1, bx, by), labels.reshape(-1, bx, by)

    def trio(tall, wide):
        kinds = ((nvec, jnp.float32), (3, jnp.float32), (4, jnp.int32))
        return tuple(pltpu.VMEM((2, depth, tall, wide), kind) for depth, kind in kinds)

    dma = pltpu.SemaphoreType.DMA
    anywhere, inside = pl.BlockSpec(memory_space=pl.ANY), pl.BlockSpec(memory_space=pltpu.VMEM)
    return pl.pallas_call(
        whole_kernel,
        in_specs=[anywhere] * 7 + [inside] * 2,
        out_specs=anywhere,
        out_shape=jax.ShapeDtypeStruct(q.shape, jnp.float32),
        scratch_shapes=[
            lines, packed, packed, packed, lines, pltpu.VMEM((4,) + mats.shape, jnp.bfloat16),
            pltpu.VMEM(q.shape, jnp.float32), trio(RIM, by), trio(bx, 128),
            pltpu.VMEM((4, bx + 2 * RIM, 128), jnp.float32),
            trio(STRIP + 2 * RIM, by),
            dma((4,)), dma((nvec,)), dma((chunks, along)), dma((chunks,)), dma((chunks,)),
            dma((nvec,)), dma((nvec,)), dma((chunks,)), dma((chunks,)), dma((chunks,)),
            dma((chunks,)), dma((2, 3)), dma((2, 3)), dma((2, 3)), dma((2,)), dma((2,)), dma((2, 3)),
        ],
        compiler_params=pltpu.CompilerParams(
            vmem_limit_bytes=VMEM_BYTES, collective_id=0, has_side_effects=True
        ),
        cost_estimate=cost(36 * mats.size * nvec * bx * by // length, 64 * nvec * bx * by),
        name="whole",
    )(q, levels, labels, fhi, flo, thi, tlo, ky, kx)


RIM = 8
VMEM_BYTES = 60 * 2**20


STRIP = 32


def data_strip(fields, nvec):
    tall, wide = fields[0].shape

    def rim(f):
        return (pltpu.roll(f, 1, 0) + pltpu.roll(f, tall - 1, 0)) + (
            pltpu.roll(f, 1, 1) + pltpu.roll(f, wide - 1, 1)
        )

    def inverse_capacity(label):
        return jnp.where(label == 2.0, 0.25, jnp.where(label == 3.0, 0.8, 1.0))

    def conduct(label, level):
        base = jnp.where(
            label == 1.0, 1.0, jnp.where(label == 2.0, 0.6, jnp.where(label == 3.0, 0.35, 0.0))
        )
        return TIME_STEP * base * (1.0 + 0.5 * jnp.tanh(level))

    label = fields[nvec : nvec + 4]
    level = fields[nvec + 4 :]
    ic_top0, ic_top1 = inverse_capacity(label[0]), inverse_capacity(label[2])
    ic_low1 = inverse_capacity(label[3])
    c_top0, c_low0 = conduct(label[0], level[0]), conduct(label[1], level[1])
    c_top1 = conduct(label[2], level[2])
    out = []
    for q in fields[:nvec]:
        first_u = TIME_STEP * q * ic_top0
        second_top = (2.0 * TIME_STEP) * q + c_top0 * (rim(first_u) - 6.0 * first_u)
        top_u = second_top * ic_top1
        low_u = c_low0 * first_u * ic_low1
        third_top = second_top + c_top1 * (rim(top_u) - 6.0 * top_u + low_u) + TIME_STEP * q
        adj_three = OBS_WEIGHT * third_top * ic_top1 * ic_top1
        push_top = c_top1 * adj_three
        adj_two = adj_three + (rim(push_top) - 6.0 * push_top) * ic_top1
        pull_top = c_top0 * adj_two
        pull_low = c_low0 * (push_top * ic_low1)
        adj_one = adj_two + (rim(pull_top) - 6.0 * pull_top + pull_low) * ic_top0
        out.append(TIME_STEP * (adj_three + adj_two + adj_one))
    return out


def shards(q, heat, labels):
    nvec, bx, by = q.shape
    along, across = lax.axis_size("gy"), lax.axis_size("gx")
    rows, width = bx // along, by // across
    square = bx * across == by * along
    if not square or rows % 16 or width % 128 or by % (by * along // OUTER) or bx % (STRIP * nvec):
        return shards_general(q, heat, labels)
    return whole(q, heat, labels)


def solution(mesh):
    in_specs = (P(None, "gx", "gy"), P(None, None, "gx", "gy"), P(None, None, "gx", "gy"))
    out_specs = P(None, "gx", "gy")
    return jax.shard_map(shards, mesh=mesh, in_specs=in_specs, out_specs=out_specs, check_vma=False)
```

```python
import math

import jax
import jax.numpy as jnp
import numpy as np
from jax import lax
from jax.experimental import pallas as pl
from jax.experimental.pallas import tpu as pltpu
from jax.sharding import PartitionSpec as P

TIME_STEP = 0.1
OBS_WEIGHT = 10.0
PRIOR_GAIN = 0.005
HIGHEST = lax.Precision.HIGHEST


def with_halo(cells, sides, width):
    for axis, dim in sides:
        count = lax.axis_size(axis)
        ends = count - 1
        head = lax.slice_in_dim(cells, 0, width, axis=dim)
        tail = lax.slice_in_dim(cells, cells.shape[dim] - width, cells.shape[dim], axis=dim)
        cells = jnp.concatenate(
            [
                lax.ppermute(tail, axis, [(i, (i + 1) % count) for i in range(ends)]),
                cells,
                lax.ppermute(head, axis, [((i + 1) % count, i) for i in range(ends)]),
            ],
            axis=dim,
        )
    return cells


def surface_rim(field):
    padded = with_halo(field, (("gx", 1), ("gy", 2)), 1)
    return padded[:, 2:, 1:-1] + padded[:, :-2, 1:-1] + padded[:, 1:-1, 2:] + padded[:, 1:-1, :-2]


def cos_sin(horizontal_line_total, col_count, modulus):
    row_ids = jnp.arange(horizontal_line_total, dtype=jnp.int32)[:, None]
    col_ids = jnp.arange(col_count, dtype=jnp.int32)[None, :]
    angles = (row_ids * col_ids % modulus).astype(jnp.float32) * (2.0 * math.pi / modulus)
    return (jnp.cos(angles), jnp.sin(angles))


def tables(length):
    bit_count = length.bit_length() - 1
    outer_len = 2 ** (bit_count // 2)
    inner_len = length // outer_len
    cos_outer, sin_outer = cos_sin(outer_len, outer_len, outer_len)
    cos_inner, sin_inner = cos_sin(inner_len, inner_len, inner_len)
    twist_cos, twist_sin = cos_sin(outer_len, inner_len, length)
    outer_fwd = jnp.stack([cos_outer, -sin_outer])
    inner_fwd = jnp.stack([jnp.stack([cos_inner, -sin_inner]), jnp.stack([sin_inner, cos_inner])])
    inner_inv = jnp.stack([jnp.stack([cos_inner, sin_inner]), jnp.stack([-sin_inner, cos_inner])])
    outer_inv = jnp.stack([cos_outer, -sin_outer])
    freq_index = (
        jnp.arange(outer_len, dtype=jnp.int32)[:, None]
        + outer_len * jnp.arange(inner_len, dtype=jnp.int32)[None, :]
    )
    signed = jnp.where(freq_index < length // 2, freq_index, freq_index - length).astype(
        jnp.float32
    )
    wave_sq = (signed * (2.0 * math.pi / length)) ** 2
    return (
        length,
        outer_len,
        inner_len,
        outer_fwd,
        inner_fwd,
        inner_inv,
        outer_inv,
        twist_cos,
        twist_sin,
        wave_sq,
    )


def forward(field, table):
    (
        length,
        outer_len,
        inner_len,
        outer_fwd,
        inner_fwd,
        inner_inv,
        outer_inv,
        twist_cos,
        twist_sin,
        wave_sq,
    ) = table
    grid = field.reshape(field.shape[:-1] + (outer_len, inner_len))
    stepped = jnp.einsum("...ab,rak->...rkb", grid, outer_fwd, precision=HIGHEST)
    step_re = stepped[..., 0, :, :]
    step_im = stepped[..., 1, :, :]
    twisted = jnp.stack(
        [step_re * twist_cos + step_im * twist_sin, step_im * twist_cos - step_re * twist_sin],
        axis=-3,
    )
    spec = jnp.einsum("...rkb,rsbm->...skm", twisted, inner_fwd, precision=HIGHEST)
    return (spec[..., 0, :, :], spec[..., 1, :, :])


def inverse(spec_re, spec_im, table):
    (
        length,
        outer_len,
        inner_len,
        outer_fwd,
        inner_fwd,
        inner_inv,
        outer_inv,
        twist_cos,
        twist_sin,
        wave_sq,
    ) = table
    stacked = jnp.stack([spec_re, spec_im], axis=-3)
    halved = jnp.einsum("...skm,srbm->...rkb", stacked, inner_inv, precision=HIGHEST)
    half_re = halved[..., 0, :, :]
    half_im = halved[..., 1, :, :]
    turned = jnp.stack(
        [half_re * twist_cos - half_im * twist_sin, half_im * twist_cos + half_re * twist_sin],
        axis=-3,
    )
    grid = jnp.einsum("...rkb,rka->...ab", turned, outer_inv, precision=HIGHEST)
    return grid.reshape(grid.shape[:-2] + (length,)) / length


def shards_general(flux_perturbation, archived_nominal_heat_levels, archived_solidity_labels):
    capacity = jnp.where(
        archived_solidity_labels == 0, 1.0, jnp.where(archived_solidity_labels == 1, 4.0, 1.25)
    ).astype(jnp.float32)
    diffusion_advance = jnp.where(
        archived_solidity_labels == 0, 1.0, jnp.where(archived_solidity_labels == 1, 0.6, 0.35)
    ).astype(jnp.float32)
    diffusion_advance = diffusion_advance * (1.0 + 0.5 * jnp.tanh(archived_nominal_heat_levels))
    rows = lax.all_to_all(flux_perturbation, "gx", split_axis=2, concat_axis=1, tiled=True)
    row_table = tables(rows.shape[1])
    first_u = TIME_STEP * flux_perturbation / capacity[0, 0]
    second_top = TIME_STEP * flux_perturbation + TIME_STEP * (
        diffusion_advance[0, 0] * (surface_rim(first_u) - 6.0 * first_u) + flux_perturbation
    )
    second_low = TIME_STEP * diffusion_advance[0, 1] * first_u
    top_u = second_top / capacity[1, 0]
    low_u = second_low / capacity[1, 1]
    third_top = second_top + TIME_STEP * (
        diffusion_advance[1, 0] * (surface_rim(top_u) - 6.0 * top_u + low_u) + flux_perturbation
    )
    misfit = OBS_WEIGHT * third_top / capacity[1, 0]
    adj_three = misfit / capacity[1, 0]
    push_top = TIME_STEP * diffusion_advance[1, 0] * adj_three
    adj_two_top = adj_three + (surface_rim(push_top) - 6.0 * push_top) / capacity[1, 0]
    adj_two_low = push_top / capacity[1, 1]
    pull_top = TIME_STEP * diffusion_advance[0, 0] * adj_two_top
    pull_low = TIME_STEP * diffusion_advance[0, 1] * adj_two_low
    adj_one_top = adj_two_top + (surface_rim(pull_top) - 6.0 * pull_top + pull_low) / capacity[0, 0]
    data_term = TIME_STEP * (adj_three + adj_two_top + adj_one_top)
    row_re, row_im = forward(jnp.swapaxes(rows, 1, 2), row_table)
    wave_x = row_table[-1]
    second_x = jnp.swapaxes(
        inverse(2.0 * PRIOR_GAIN * wave_x * row_re, 2.0 * PRIOR_GAIN * wave_x * row_im, row_table),
        1,
        2,
    )
    fourth_x = jnp.swapaxes(
        inverse(
            PRIOR_GAIN * wave_x * wave_x * row_re, PRIOR_GAIN * wave_x * wave_x * row_im, row_table
        ),
        1,
        2,
    )
    second_back, fourth_part = (
        lax.all_to_all(second_x, "gx", split_axis=1, concat_axis=2, tiled=True),
        lax.all_to_all(fourth_x, "gx", split_axis=1, concat_axis=2, tiled=True),
    )
    cols_dir, cols_second = (
        lax.all_to_all(flux_perturbation, "gy", split_axis=1, concat_axis=2, tiled=True),
        lax.all_to_all(second_back, "gy", split_axis=1, concat_axis=2, tiled=True),
    )
    col_table = tables(cols_dir.shape[2])
    dir_re, dir_im = forward(cols_dir, col_table)
    sec_re, sec_im = forward(cols_second, col_table)
    wave_y = col_table[-1]
    mixed = inverse(
        PRIOR_GAIN * wave_y * wave_y * dir_re + wave_y * sec_re,
        PRIOR_GAIN * wave_y * wave_y * dir_im + wave_y * sec_im,
        col_table,
    )
    mixed_back = lax.all_to_all(mixed, "gy", split_axis=2, concat_axis=1, tiled=True)
    return data_term + fourth_part + mixed_back


OUTER = 16


def half_spectrum(xs):
    n = len(xs)
    if n == 2:
        return [(xs[0] + xs[1], None), (xs[0] - xs[1], None)]
    even, odd = half_spectrum(xs[0::2]), half_spectrum(xs[1::2])
    out = [None] * (n // 2 + 1)
    for k in range(n // 4 + 1):
        er, ei = even[k]
        orr, oi = odd[k]
        if k == 0:
            out[0] = (er + orr, None)
            out[n // 2] = (er - orr, None)
        elif k == n // 4:
            out[k] = (er, -orr)
        else:
            c, s = math.cos(2 * math.pi * k / n), math.sin(2 * math.pi * k / n)
            if 8 * k == n:
                tr, ti = c * (orr + oi), c * (oi - orr)
            else:
                tr, ti = c * orr + s * oi, c * oi - s * orr
            out[k] = (er + tr, ei + ti)
            out[n // 2 - k] = (er - tr, ti - ei)
    return out


def half_spectrum_t(gs):
    half = len(gs) - 1
    n = 2 * half
    if n == 2:
        return [gs[0][0] + gs[1][0], gs[0][0] - gs[1][0]]
    even, odd = [], []
    for m in range(n // 4 + 1):
        gr, gi = gs[m]
        if m == 0:
            hr = gs[half][0]
            even.append((gr + hr, None))
            odd.append((gr - hr, None))
        elif m == n // 4:
            even.append((gr, None))
            odd.append((-gi, None))
        else:
            hr, hi = gs[half - m]
            even.append((gr + hr, gi - hi))
            dr, di = gr - hr, gi + hi
            c, s = math.cos(2 * math.pi * m / n), math.sin(2 * math.pi * m / n)
            if 8 * m == n:
                odd.append((c * (dr - di), c * (dr + di)))
            else:
                odd.append((c * dr - s * di, c * di + s * dr))
    out = [None] * n
    out[0::2] = half_spectrum_t(even)
    out[1::2] = half_spectrum_t(odd)
    return out


def line_tables(length):
    inner = length // OUTER
    groups = OUTER // 2
    b = np.arange(inner)[:, None]
    mats = np.zeros((groups, 2 * inner, 2 * inner))
    freq = np.zeros((groups, 2 * inner), np.int64)
    scale = math.sqrt(2.0 / length)
    for k1 in range(1, groups):
        k = k1 + OUTER * np.arange(inner)
        angle = 2.0 * math.pi * ((b * k[None, :]) % length) / length
        c, s = np.cos(angle) * scale, np.sin(angle) * scale
        mats[k1 - 1] = np.block([[c, -s], [s, c]])
        freq[k1 - 1] = np.concatenate([k, k])
    last = groups - 1
    for part, first in ((0, 0), (1, groups)):
        k = first + OUTER * np.arange(inner // 2)
        angle = 2.0 * math.pi * ((b * k[None, :]) % length) / length
        c, s = np.cos(angle) * scale, np.sin(angle) * scale
        k_sin = k.copy()
        if first == 0:
            c[:, 0] = math.sqrt(1.0 / length)
            k_sin[0] = length // 2
            s[:, 0] = -math.sqrt(1.0 / length) * (1 - 2 * (np.arange(inner) % 2))
        span = slice(part * inner, (part + 1) * inner)
        mats[last][span, span] = np.concatenate([c, -s], axis=1)
        freq[last][span] = np.concatenate([k, k_sin])
    signed = np.where(freq < length // 2, freq, freq - length)
    wave = (signed * (2.0 * math.pi / length)) ** 2
    return mats, wave


def two_parts(mats):
    top = np.asarray(mats, np.float32).astype(jnp.bfloat16)
    rest = (np.asarray(mats, np.float64) - top.astype(np.float64)).astype(jnp.bfloat16)
    return top, rest


def split(x):
    top = x.astype(jnp.bfloat16)
    return top, (x - top.astype(jnp.float32)).astype(jnp.bfloat16)


def dot32(a, b):
    return jnp.dot(a, b, preferred_element_type=jnp.float32)


def right(x, hi, lo):
    top, rest = split(x)
    both = dot32(jnp.concatenate([top, rest], axis=0), hi)
    return both[: x.shape[0]] + (both[x.shape[0] :] + dot32(top, lo))


def left(hi, lo, x):
    top, rest = split(x)
    both = dot32(hi, jnp.concatenate([top, rest], axis=1))
    return both[:, : x.shape[1]] + (dot32(lo, top) + both[:, x.shape[1] :])


def pairs(spec):
    ends = len(spec) - 1
    return [spec[k] for k in range(1, ends)] + [(spec[0][0], spec[ends][0])]


def unpairs(groups):
    return [(groups[-1][0], None)] + groups[:-1] + [(groups[-1][1], None)]


MESH = pl.DeviceIdType.MESH
CUTS = 8
LEAD = 16
PACK_AT = 3
STRIPS_AT = 16
X_AT = 18
X_STEP = 14
BACK_AT = 28
LAG = 4


def y_forward(lines, v, rows, mats, spec):
    wide, width = lines.shape[-1], spec.shape[-1]
    inner = lines.shape[1] * wide // OUTER
    per = wide // inner
    xs = [lines[v, a // per, rows, (a % per) * inner : (a % per + 1) * inner] for a in range(OUTER)]
    each = 2 * inner // width
    for g, (re, im) in enumerate(pairs(half_spectrum(xs))):
        res = right(jnp.concatenate([re, im], axis=1), mats[0, g], mats[1, g])
        for c in range(each):
            spec[v, g * each + c, rows] = res[:, c * width : (c + 1) * width]


def y_inverse(backs, v, rows, mats, lines):
    wide, width = lines.shape[-1], backs.shape[-1]
    inner = lines.shape[1] * wide // OUTER
    per = wide // inner
    each = 2 * inner // width
    groups = []
    for g in range(OUTER // 2):
        spec = jnp.concatenate([backs[v, g * each + c, rows] for c in range(each)], axis=1)
        res = right(spec, mats[2, g], mats[3, g])
        groups.append((res[:, :inner], res[:, inner:]))
    for a, slab in enumerate(half_spectrum_t(unpairs(groups))):
        lines[v, a // per, rows, (a % per) * inner : (a % per + 1) * inner] = slab


def wave_of(g, inner, width, length):
    row = lax.broadcasted_iota(jnp.int32, (2 * inner, width), 0)
    place = row % inner
    if g < OUTER // 2 - 1:
        k = g + 1 + OUTER * place
    else:
        k = jnp.where(row < inner, 0, OUTER // 2) + OUTER * (place % (inner // 2))
        k = jnp.where(row == inner // 2, length // 2, k)
    k = jnp.where(k < length // 2, k, k - length).astype(jnp.float32) * (2.0 * math.pi / length)
    return k * k


def x_apply(full, v, ky, mats, out):
    count, rows, width = full.shape[1:]
    inner = count * rows // OUTER
    per = inner // rows
    slabs = [full[v, a * per : (a + 1) * per].reshape(inner, width) for a in range(OUTER)]
    groups = []
    for g, (re, im) in enumerate(pairs(half_spectrum(slabs))):
        spec = left(mats[2, g], mats[3, g], jnp.concatenate([re, im], axis=0))
        wave = wave_of(g, inner, width, count * rows) + ky
        res = left(mats[0, g], mats[1, g], PRIOR_GAIN * wave * wave * spec)
        groups.append((res[:inner], res[inner:]))
    for a, res in enumerate(half_spectrum_t(unpairs(groups))):
        out[v, a * per : (a + 1) * per] = res.reshape(per, rows, width)


def settle(ref, sem):
    pltpu.make_async_copy(ref, ref, sem).wait()


def whole_kernel(
    q_ref, heat_ref, labels_ref, fhi_ref, flo_ref, thi_ref, tlo_ref, ky_ref, data,
    lines, spec, full, backs, last, mats, ends, edges, packs, strips,
    mat_sem, own_sem, send_lines, get_lines, send_full, get_full,
    send_backs, get_backs, send_last, get_last,
    send_ends, get_ends, edge_sem, send_packs, get_packs, strip_sem,
):
    across, along = lax.axis_size("gx"), lax.axis_size("gy")
    gx, gy = lax.axis_index("gx"), lax.axis_index("gy")
    count, me = across * along, gx * along + gy
    nvec, bx, by = q_ref.shape
    tall = bx // along
    step = tall // CUTS
    chunks = nvec * CUTS

    def where(p):
        return (lax.div(p, along), lax.rem(p, along))

    def span(c):
        return lax.div(c, CUTS), pl.multiple_of(lax.rem(c, CUTS) * step, step)

    def each(total, body):
        def run(i, carry):
            body(i)
            return carry

        lax.fori_loop(0, total, run, 0)

    def own_lines(v):
        return pltpu.make_async_copy(
            q_ref.at[v, pl.ds(pl.multiple_of(gy * tall, tall), tall)], lines.at[v, gy],
            own_sem.at[v],
        )

    loads = [
        pltpu.make_async_copy(ref, mats.at[i], mat_sem.at[i])
        for i, ref in enumerate((fhi_ref, flo_ref, thi_ref, tlo_ref))
    ]
    each(nvec, lambda v: own_lines(v).start())
    for load in loads[:2]:
        load.start()
    barrier = pltpu.get_barrier_semaphore()

    def greet(i):
        p = lax.rem(me + 1 + i, count)
        pl.semaphore_signal(barrier, inc=1, device_id=where(p), device_id_type=MESH)

    each(count - 1, greet)
    pl.semaphore_wait(barrier, count - 1)

    def start_lines(c):
        v, first = span(c)

        def one(i):
            p = lax.rem(gy + 1 + i, along)
            pltpu.make_async_remote_copy(
                q_ref.at[v, pl.ds(pl.multiple_of(p * tall + first, step), step)],
                lines.at[v, gy, pl.ds(first, step)],
                send_lines.at[c], get_lines.at[c],
                device_id=(gx, p), device_id_type=MESH,
            ).start()

        each(along - 1, one)

    start_lines(0)
    sources = (q_ref, heat_ref, labels_ref)

    def end_copy(side, kind, target):
        src, dst = sources[kind], ends[kind]
        first = bx - RIM if side == 0 else 0
        return pltpu.make_async_remote_copy(
            src.at[pl.ds(0, dst.shape[1]), pl.ds(first, RIM)], dst.at[side],
            send_ends.at[side, kind], get_ends.at[side, kind],
            device_id=(target, gy), device_id_type=MESH,
        )

    def edge_copy(side, kind):
        src, dst = sources[kind], edges[kind]
        return pltpu.make_async_copy(
            src.at[pl.ds(0, dst.shape[0]), :, pl.ds(by - 128 if side else 0, 128)], dst,
            edge_sem.at[side, kind],
        )

    for side, (sends, target) in enumerate(((gx < across - 1, gx + 1), (gx > 0, gx - 1))):

        @pl.when(sends)
        def _():
            for kind in range(3):
                end_copy(side, kind, target).start()

        @pl.when(gx == (0 if side == 0 else across - 1))
        def _():
            for kind in range(3):
                ref = ends[kind]
                ref[side] = jnp.full(ref.shape[1:], -1 if kind == 2 else 0, ref.dtype)

        @pl.when(gy == (along - 1 if side == 0 else 0))
        def _():
            packs[2 + side] = jnp.zeros(packs.shape[1:], jnp.float32)

    each(LEAD - 1, lambda c: start_lines(c + 1))
    for load in loads[:2]:
        load.wait()
    each(nvec, lambda v: own_lines(v).wait())
    for kind in range(3):
        edge_copy(0, kind).start()
    for load in loads[2:]:
        load.start()

    def scatter(src, dst, v, first, send, get):
        rows = pl.ds(first, step)
        dst[v, me, rows] = src[v, me, rows]

        def one(i):
            p = lax.rem(me + 1 + i, count)
            pltpu.make_async_remote_copy(
                src.at[v, p, rows], dst.at[v, me, rows], send, get,
                device_id=where(p), device_id_type=MESH,
            ).start()

        each(count - 1, one)

    def forward_y(c):
        v, first = span(c)
        rows = pl.ds(first, step)
        settle(lines.at[v, pl.ds(0, along - 1), rows], get_lines.at[c])

        @pl.when(c + LEAD < chunks)
        def _():
            start_lines(c + LEAD)

        y_forward(lines, v, rows, mats, spec)
        scatter(spec, full, v, first, send_full.at[v], get_full.at[v])

    def packed(side, fields):
        lane = lax.broadcasted_iota(jnp.int32, fields[0].shape, 1)
        total = jnp.zeros(fields[0].shape, jnp.float32)
        for i, f in enumerate(fields):
            moved = pltpu.roll(f, RIM * (i + side), 1)
            total = jnp.where((lane >= RIM * i) & (lane < RIM * (i + 1)), moved, total)
        return total

    def nine(q, level, label):
        return (
            [q(v) for v in range(nvec)]
            + [(label(i) + 1).astype(jnp.float32) for i in range(4)]
            + [level(i) for i in range(3)]
        )

    def pack_copy(side, target):
        return pltpu.make_async_remote_copy(
            packs.at[side], packs.at[2 + side], send_packs.at[side], get_packs.at[side],
            device_id=(gx, target), device_id_type=MESH,
        )

    total = bx // STRIP
    strip_tall = STRIP + 2 * RIM

    def strip_copy(s, slot):
        for kind in range(3):
            src, dst, sem = sources[kind], strips[kind], strip_sem.at[slot, kind]
            depth = pl.ds(0, dst.shape[1])

            @pl.when((s > 0) & (s < total - 1))
            def _():
                rows = pl.ds(pl.multiple_of(s * STRIP - RIM, RIM), strip_tall)
                pltpu.make_async_copy(src.at[depth, rows], dst.at[slot], sem).start()

            for edge, side, near_at, far_at, from_at in (
                (0, 0, 0, RIM, 0),
                (total - 1, 1, STRIP + RIM, 0, bx - STRIP - RIM),
            ):

                @pl.when(s == edge)
                def _():
                    pltpu.make_async_copy(
                        ends[kind].at[side], dst.at[slot, :, pl.ds(near_at, RIM)], sem
                    ).start()
                    pltpu.make_async_copy(
                        src.at[depth, pl.ds(from_at, STRIP + RIM)],
                        dst.at[slot, :, pl.ds(far_at, STRIP + RIM)],
                        sem,
                    ).start()

    def strip_work(s):
        slot = lax.rem(s, 2)
        for kind in range(3):
            settle(strips[kind].at[slot], strip_sem.at[slot, kind])

        @pl.when(s + 1 < total)
        def _():
            strip_copy(s + 1, 1 - slot)

        first = pl.multiple_of(s * STRIP, STRIP)
        over, under = (packs[side, pl.ds(first, strip_tall)] for side in (2, 3))
        lane = lax.broadcasted_iota(jnp.int32, over.shape, 1)

        def side_of(i):
            return jnp.where(
                lane < RIM,
                pltpu.roll(over, (128 - RIM * i) % 128, 1),
                jnp.where(lane >= 128 - RIM, pltpu.roll(under, 128 - RIM - RIM * i, 1), 0.0),
            )

        middle = nine(*[lambda i, r=r: r[slot, i] for r in strips])
        fields = [jnp.concatenate([f, side_of(i)], axis=1) for i, f in enumerate(middle)]
        for v, res in enumerate(data_strip(fields, nvec)):
            data[v, pl.ds(first, STRIP)] = res[RIM : RIM + STRIP, :by]

    def pack_edges():
        for side, gets in enumerate((gx > 0, gx < across - 1)):

            @pl.when(gets)
            def _():
                for kind in range(3):
                    settle(ends[kind].at[side], get_ends.at[side, kind])

        for side in range(2):
            for kind in range(3):
                edge_copy(side, kind).wait()
            cols = slice(by - 128, by) if side else slice(0, 128)
            for end, at in ((0, 0), (1, RIM + bx)):
                packs[side, at : at + RIM] = packed(
                    side, nine(*[lambda i, r=r: r[end, i, :, cols] for r in ends])
                )

            def pack_some(n):
                first = pl.multiple_of(n * 64, 64)
                packs[side, pl.ds(pl.multiple_of(first + RIM, RIM), 64)] = packed(
                    side, nine(*[lambda i, r=r: r[i, pl.ds(first, 64)] for r in edges])
                )

            each(bx // 64, pack_some)
            for kind in range(3 if side == 0 else 0):
                edge_copy(1, kind).start()

        for side, (sends, target) in enumerate(((gy > 0, gy - 1), (gy < along - 1, gy + 1))):

            @pl.when(sends)
            def _():
                pack_copy(side, target).start()
        strip_copy(jnp.int32(0), 0)

    def get_edges():
        for side, gets in enumerate((gy < along - 1, gy > 0)):

            @pl.when(gets)
            def _():
                settle(packs.at[2 + side], get_packs.at[side])

    def along_x(v):
        @pl.when(v == 0)
        def _():
            for load in loads[2:]:
                load.wait()

        settle(full.at[v, pl.ds(0, count - 1)], get_full.at[v])
        settle(spec.at[v, pl.ds(0, count - 1)], send_full.at[v])
        x_apply(full, v, ky_ref[pl.ds(me, 1)], mats, spec)

        def part(h):
            c = v * CUTS + h
            first = pl.multiple_of(h * step, step)
            scatter(spec, backs, v, first, send_backs.at[c], get_backs.at[c])

        each(CUTS, part)

    def finish(c):
        v, first = span(c)
        settle(last.at[v, pl.ds(0, along - 1), pl.ds(first, step)], get_last.at[c])

        def one(s):
            rows = pl.ds(pl.multiple_of(s * tall + first, step), step)
            data[v, rows] = data[v, rows] + last[v, s, pl.ds(first, step)]

        each(along, one)

    def backward_y(c):
        v, first = span(c)
        rows = pl.ds(first, step)
        settle(backs.at[v, pl.ds(0, count - 1), rows], get_backs.at[c])
        y_inverse(backs, v, rows, mats, lines)
        last[v, gy, rows] = lines[v, gy, rows]

        def one(i):
            p = lax.rem(gy + 1 + i, along)
            pltpu.make_async_remote_copy(
                lines.at[v, p, rows], last.at[v, gy, rows], send_last.at[c], get_last.at[c],
                device_id=(gx, p), device_id_type=MESH,
            ).start()

        each(along - 1, one)

    def tick(t):
        pl.when(t < chunks)(lambda: forward_y(t))
        pl.when(t == PACK_AT)(pack_edges)
        pl.when(t == STRIPS_AT)(get_edges)
        pl.when((t >= STRIPS_AT) & (t < STRIPS_AT + total))(lambda: strip_work(t - STRIPS_AT))
        pl.when((t >= X_AT) & (t < X_AT + X_STEP * nvec) & (lax.rem(t - X_AT, X_STEP) == 0))(
            lambda: along_x(lax.div(t - X_AT, X_STEP))
        )
        pl.when((t >= BACK_AT) & (t < BACK_AT + chunks))(lambda: backward_y(t - BACK_AT))
        pl.when(t >= BACK_AT + LAG)(lambda: finish(t - BACK_AT - LAG))

    each(BACK_AT + chunks + LAG, tick)

    def drain(c):
        v, first = span(c)
        rows = pl.ds(first, step)
        settle(lines.at[v, pl.ds(0, along - 1), rows], send_lines.at[c])
        settle(lines.at[v, pl.ds(0, along - 1), rows], send_last.at[c])
        settle(spec.at[v, pl.ds(0, count - 1), rows], send_backs.at[c])

    each(chunks, drain)
    for side, sends in enumerate((gx < across - 1, gx > 0)):

        @pl.when(sends)
        def _():
            for kind in range(3):
                settle(ends[kind].at[side], send_ends.at[side, kind])

    for side, sends in enumerate((gy > 0, gy < along - 1)):

        @pl.when(sends)
        def _():
            settle(packs.at[side], send_packs.at[side])


def cost(flops, moved):
    return pl.CostEstimate(flops=int(flops), bytes_accessed=int(moved), transcendentals=0)


def whole(q, heat, labels):
    across, along = lax.axis_size("gx"), lax.axis_size("gy")
    nvec, bx, by = q.shape
    length = by * along
    count = across * along
    rows = bx // along
    width = length // count
    mats, wave = line_tables(length)
    fhi, flo = two_parts(mats)
    thi, tlo = two_parts(np.swapaxes(mats, 1, 2))
    ky = jnp.asarray(wave.reshape(count, width), jnp.float32)
    lines = pltpu.VMEM((nvec, along, rows, by), jnp.float32)
    packed = pltpu.VMEM((nvec, count, rows, width), jnp.float32)
    chunks = nvec * CUTS
    levels, labels = heat.reshape(-1, bx, by), labels.reshape(-1, bx, by)

    def trio(copies, tall, wide):
        kinds = ((nvec, jnp.float32), (3, jnp.float32), (4, jnp.int32))
        return tuple(pltpu.VMEM(copies + (depth, tall, wide), kind) for depth, kind in kinds)

    dma = pltpu.SemaphoreType.DMA
    anywhere, inside = pl.BlockSpec(memory_space=pl.ANY), pl.BlockSpec(memory_space=pltpu.VMEM)
    return pl.pallas_call(
        whole_kernel,
        in_specs=[anywhere] * 7 + [inside],
        out_specs=inside,
        out_shape=pltpu.VMEM(q.shape, jnp.float32),
        scratch_shapes=[
            lines, packed, packed, packed, lines, pltpu.VMEM((4,) + mats.shape, jnp.bfloat16),
            trio((2,), RIM, by), trio((), bx, 128),
            pltpu.VMEM((4, bx + 2 * RIM, 128), jnp.float32),
            trio((2,), STRIP + 2 * RIM, by),
            dma((4,)), dma((nvec,)), dma((chunks,)), dma((chunks,)),
            dma((nvec,)), dma((nvec,)), dma((chunks,)), dma((chunks,)), dma((chunks,)),
            dma((chunks,)), dma((2, 3)), dma((2, 3)), dma((2, 3)), dma((2,)), dma((2,)), dma((2, 3)),
        ],
        compiler_params=pltpu.CompilerParams(
            vmem_limit_bytes=VMEM_BYTES, collective_id=0, has_side_effects=True
        ),
        cost_estimate=cost(36 * mats.size * nvec * bx * by // length, 64 * nvec * bx * by),
        name="whole",
    )(q, levels, labels, fhi, flo, thi, tlo, ky)


RIM = 8
VMEM_BYTES = 52 * 2**20


STRIP = 32


def data_strip(fields, nvec):
    tall, wide = fields[0].shape

    def rim(f):
        return (pltpu.roll(f, 1, 0) + pltpu.roll(f, tall - 1, 0)) + (
            pltpu.roll(f, 1, 1) + pltpu.roll(f, wide - 1, 1)
        )

    def inverse_capacity(label):
        return jnp.where(label == 2.0, 0.25, jnp.where(label == 3.0, 0.8, 1.0))

    def conduct(label, level):
        base = jnp.where(
            label == 1.0, 1.0, jnp.where(label == 2.0, 0.6, jnp.where(label == 3.0, 0.35, 0.0))
        )
        return TIME_STEP * base * (1.0 + 0.5 * jnp.tanh(level))

    label = fields[nvec : nvec + 4]
    level = fields[nvec + 4 :]
    ic_top0, ic_top1 = inverse_capacity(label[0]), inverse_capacity(label[2])
    ic_low1 = inverse_capacity(label[3])
    c_top0, c_low0 = conduct(label[0], level[0]), conduct(label[1], level[1])
    c_top1 = conduct(label[2], level[2])
    out = []
    for q in fields[:nvec]:
        first_u = TIME_STEP * q * ic_top0
        second_top = (2.0 * TIME_STEP) * q + c_top0 * (rim(first_u) - 6.0 * first_u)
        top_u = second_top * ic_top1
        low_u = c_low0 * first_u * ic_low1
        third_top = second_top + c_top1 * (rim(top_u) - 6.0 * top_u + low_u) + TIME_STEP * q
        adj_three = OBS_WEIGHT * third_top * ic_top1 * ic_top1
        push_top = c_top1 * adj_three
        adj_two = adj_three + (rim(push_top) - 6.0 * push_top) * ic_top1
        pull_top = c_top0 * adj_two
        pull_low = c_low0 * (push_top * ic_low1)
        adj_one = adj_two + (rim(pull_top) - 6.0 * pull_top + pull_low) * ic_top0
        out.append(TIME_STEP * (adj_three + adj_two + adj_one))
    return out


def shards(q, heat, labels):
    nvec, bx, by = q.shape
    along, across = lax.axis_size("gy"), lax.axis_size("gx")
    rows, width = bx // along, by // across
    square = bx * across == by * along
    split = nvec == 2 and rows % (16 * CUTS) == 0 and width % 128 == 0 and bx % 64 == 0
    early = bx // STRIP <= BACK_AT + LAG - STRIPS_AT
    if not (square and split and early) or by % (by * along // OUTER):
        return shards_general(q, heat, labels)
    return whole(q, heat, labels)


def solution(mesh):
    in_specs = (P(None, "gx", "gy"), P(None, None, "gx", "gy"), P(None, None, "gx", "gy"))
    out_specs = P(None, "gx", "gy")
    return jax.shard_map(shards, mesh=mesh, in_specs=in_specs, out_specs=out_specs, check_vma=False)
```
